32 devices in a mesh: parts: 2 (over y), tm: 8 (over z, x), band: 2 (over core).
Axes of the slice: x: 2, y: 2, z: 4, core: 2. Of those that a mesh axis runs over, the one named last changes fastest.
Arguments:
- query_tokens: bfloat16 [16, 8, 32, 2240], P(('parts', 'tm'), 'band'), parts along dimension 0, may hold values from -6 to 6
- key_tokens: bfloat16 [16, 8, 32, 2240], P(('parts', 'tm'), 'band'), parts along dimension 0, may hold values from -6 to 6
- value_tokens: bfloat16 [16, 8, 32, 2240], P(('parts', 'tm'), 'band'), parts along dimension 0, may hold values from -14 to 14
- norm_gain: float32 [2240], replicated, may hold values from 0.1 to 1.9
- out_weight: bfloat16 [2, 8, 313600], P('band', 'tm'), may hold values from -0.125 to 0.125
Outputs:
- block_out: bfloat16 [16, 8, 32, 2240], P(('parts', 'tm'), 'band'), parts along dimension 0
The draws below stay inside these ranges and needn't reach their ends.
There are 2 independent parts, one for each index of `parts`. The reference program is written for one: setup_inputs(seed, part) draws one part's arguments, and reference() takes and returns one part's arrays. A program takes and returns all parts, laid end to end along the dimension named above; an argument that names none is the same for every part. Nothing has to cross between parts.
All inputs are finite; a program needn't handle non-finite values.
Results may differ from the reference program's by a relative error of at most 0.0049.
Values may be sent and summed in bfloat16 or wider, within the bound.
A program may use at most 128 MiB of HBM per device.

```python
import math
import jax
import jax.numpy as jnp
from jax import lax

HEADS = 70
HD = 32
D = 2240
COLS = 32
FRAMES = 8
HEIGHT = 8
GROUP = 313600
N_TM = 8
N_BAND = 2


def draw_value_tokens(key, part):
    first, second = jax.random.split(jax.random.fold_in(key, 17), 2)
    channel_scale = jnp.exp(jax.random.uniform(first, (D,), jnp.float32, 0.0, math.log(10.0)))
    noise = jax.random.normal(second, (FRAMES, HEIGHT, COLS, D), jnp.float32)
    noise = jnp.clip(noise, -4.0, 4.0)
    return (noise * channel_scale / 3.0).astype(jnp.bfloat16)


def level_of(stream_key, extent, cuts, least, top_value):
    gain, own = 1.0, jax.random.fold_in(stream_key, 6)
    for dim, blocks in cuts:
        steps = jnp.exp(jax.random.uniform(jax.random.fold_in(own, dim), (blocks,), jnp.float32, least / len(cuts), top_value / len(cuts)))
        gain = gain * jnp.repeat(steps, extent[dim] // blocks).reshape([-1 if axis == dim else 1 for axis in range(len(extent))])
    return gain


def scatter_about(key, extent, scale, most, cuts=(), held_as=jnp.bfloat16):
    entries = scale * jax.random.normal(key, extent, jnp.float32)
    if cuts:
        entries = entries * level_of(key, extent, cuts, -0.22, 0.18)
    return jnp.clip(entries, -most, most).astype(held_as)


def setup_inputs(seed: int = 0, part: int = 0) -> dict:
    seeds = jax.random.split(jax.random.key(seed), 6)
    part_splits = jax.random.split(jax.random.fold_in(seeds[5], part), 6)
    query_tokens = scatter_about(part_splits[0], (FRAMES, HEIGHT, COLS, D), 1.0, 6.0, ((0, 8), (1, 2)))
    key_tokens = scatter_about(part_splits[1], (FRAMES, HEIGHT, COLS, D), 1.0, 6.0, ((0, 8), (1, 2)))
    value_tokens = draw_value_tokens(jax.random.fold_in(jax.random.fold_in(seeds[5], part), 71), part)
    norm_gain = jnp.clip(1.0 + 0.18 * jax.random.normal(seeds[3], (D,), jnp.float32), 0.1, 1.9)
    out_weight = scatter_about(seeds[4], (N_BAND, N_TM, GROUP), D ** -0.5, 0.125, ((0, 2), (1, 8)))
    return {"query_tokens": query_tokens, "key_tokens": key_tokens, "value_tokens": value_tokens, "norm_gain": norm_gain, "out_weight": out_weight}


norm_epsilon = 1e-06
read_epsilon = 1e-06

def frame_state(pieces):
    key_frame, value_frame = pieces
    key_relu = jax.nn.relu(key_frame.astype(jnp.float32)).reshape(-1, HEADS, HD)
    value_heads = value_frame.astype(jnp.float32).reshape(-1, HEADS, HD)
    state = jnp.einsum('thd,the->hde', key_relu, value_heads, precision=lax.Precision.HIGHEST)
    return (state, lax.optimization_barrier(jnp.sum(key_relu, axis=0)))

def frame_out(pieces, norm_gain, projection):
    query_frame, prefix_state, prefix_norm = pieces
    query_relu = jax.nn.relu(query_frame.astype(jnp.float32)).reshape(-1, HEADS, HD)
    numer = jnp.einsum('thd,hde->the', query_relu, prefix_state, precision=lax.Precision.HIGHEST)
    denom = jnp.einsum('thd,hd->th', query_relu, prefix_norm, precision=lax.Precision.HIGHEST) + read_epsilon
    reads = (numer / denom[:, :, None]).reshape(-1, D)
    square = lax.optimization_barrier(jnp.mean(reads * reads, axis=-1, keepdims=True))
    normed = (reads * lax.rsqrt(square + norm_epsilon) * norm_gain).astype(jnp.bfloat16)
    result = jnp.dot(normed, projection, preferred_element_type=jnp.float32)
    return result.astype(jnp.bfloat16).reshape(query_frame.shape)

def reference(query_tokens, key_tokens, value_tokens, norm_gain, out_weight):
    projection = out_weight.reshape(D, D)
    states, norms = lax.map(frame_state, (key_tokens, value_tokens))
    prefix_state = jnp.cumsum(states, axis=0)
    prefix_norm = jnp.cumsum(norms, axis=0)
    return lax.map(lambda pieces: frame_out(pieces, norm_gain, projection), (query_tokens, prefix_state, prefix_norm))
```

```python
import functools

import jax
import jax.numpy as jnp
from jax import lax
from jax.experimental import pallas as pl
from jax.experimental.pallas import tpu as pltpu
from jax.sharding import PartitionSpec as P

HEADS = 70
HD = 32
LANES = 128

norm_epsilon = 1e-06
read_epsilon = 1e-06
MESH = pl.DeviceIdType.MESH


def round_up(x, m):
    return -(-x // m) * m


def entering(x, axis):
    peers, place = (lax.axis_size(axis), lax.axis_index(axis))
    everything = jax.tree.map(lambda part: lax.all_gather(part, axis), x)

    def hop(k, before):
        return jax.tree.map(
            lambda a, part: jnp.where(k < place, a + part[k], a), before, everything
        )

    return lax.fori_loop(0, peers, hop, jax.tree.map(jnp.zeros_like, x))


def plain_body(query_tokens, key_tokens, value_tokens, norm_gain, out_weight):
    frames, rows, width, depth = query_tokens.shape
    key_relu = jax.nn.relu(key_tokens).reshape(frames, rows * width, HEADS, HD)
    value_heads = value_tokens.reshape(frames, rows * width, HEADS, HD)
    part_state = jnp.einsum(
        "fthd,fthe->fhde", key_relu, value_heads, preferred_element_type=jnp.float32
    ).reshape(frames, HEADS, HD * HD)
    part_norm = jnp.sum(key_relu, axis=1, dtype=jnp.float32)
    state_sum, norm_sum = lax.psum((part_state, part_norm), "band")
    local_state = jnp.cumsum(state_sum, axis=0)
    local_norm = jnp.cumsum(norm_sum, axis=0)
    before = entering((local_state[-1], local_norm[-1]), "tm")
    prefix_state = local_state + before[0]
    prefix_norm = local_norm + before[1]
    query_relu = jax.nn.relu(query_tokens.astype(jnp.float32)).reshape(
        frames, rows * width, HEADS, HD
    )
    numer = jnp.einsum(
        "fthd,fhde->fthe",
        query_relu,
        prefix_state.reshape(frames, HEADS, HD, HD),
        precision=lax.Precision.HIGHEST,
    )
    denom = (
        jnp.einsum("fthd,fhd->fth", query_relu, prefix_norm, precision=lax.Precision.HIGHEST)
        + read_epsilon
    )
    reads = (numer / denom[:, :, :, None]).reshape(frames * rows * width, depth)
    square = jnp.mean(reads * reads, axis=-1, keepdims=True)
    normed = (reads * lax.rsqrt(square + norm_epsilon) * norm_gain).astype(jnp.bfloat16)
    gathered = lax.all_gather(out_weight, "tm", axis=1, tiled=True)
    rows_half = gathered.reshape(-1, depth)
    result = jnp.dot(
        normed,
        lax.all_gather(rows_half, "band", axis=0, tiled=True),
        preferred_element_type=jnp.float32,
    )
    return result.astype(jnp.bfloat16).reshape(frames, rows, width, depth)


def kernel(
    n, shard_rows,
    q_ref, k_ref, v_ref, g_ref, w_ref, out_ref,
    state, own, band_out, band_in, hop_out, hop_in, final, reads,
    wbuf, abuf, acut, acc, res_out, res_in,
    w_local_sem, w_send, w_recv, s_send, s_recv, a_send, a_recv, r_send, r_recv,
):
    f32, bf16 = jnp.float32, jnp.bfloat16
    tokens, depth = q_ref.shape
    half = state.shape[2]
    block = wbuf.shape[2]
    hops = n.bit_length() - 1
    groups = -(-depth // LANES)
    per_half = half // LANES

    y, t, b = lax.axis_index("parts"), lax.axis_index("tm"), lax.axis_index("band")
    oy, ob = 1 - y, 1 - b
    mine = y * 2 + b

    def at(py, pt, pb):
        return {"parts": py, "tm": pt, "band": pb}

    odd = t % 2
    pos = (1 - odd) * (t // 2) + odd * (n - 1 - t // 2)

    def chip(p):
        p = lax.rem(p + 2 * n, n)
        back = p // (n // 2)
        return (1 - back) * (2 * p) + back * (2 * (n - 1 - p) + 1)

    right, left = chip(pos + 1), chip(pos - 1)

    barrier = pltpu.get_barrier_semaphore()
    peers = [at(y, t, ob), at(oy, t, b), at(oy, t, ob)]
    for side in (right, left):
        peers += [at(y, side, b), at(y, side, ob)]
    for s in range(hops):
        d = 1 << s
        peers += [at(y, lax.rem(t + d, n), b), at(y, lax.rem(t + n - d, n), b)]
    for peer in peers:
        pl.semaphore_signal(barrier, inc=1, device_id=peer, device_id_type=MESH)
    pl.semaphore_wait(barrier, len(peers))

    def remote(src, dst, send, recv, peer):
        return pltpu.make_async_remote_copy(
            src_ref=src, dst_ref=dst, send_sem=send, recv_sem=recv,
            device_id=peer, device_id_type=MESH,
        )

    def columns(pb):
        return w_ref.at[:, pl.ds(pl.multiple_of((y * 2 + pb) * block, LANES), block)]

    sends = []
    me_slot = b * n + t
    local = pltpu.make_async_copy(columns(b), wbuf.at[me_slot], w_local_sem)
    local.start()
    pair = remote(columns(ob), wbuf.at[me_slot], w_send.at[0], w_recv.at[me_slot], at(y, t, ob))
    pair.start()
    sends.append((None, pair))
    counter = [1]

    def w_put(src, slot, peer):
        copy = remote(src, wbuf.at[slot], w_send.at[counter[0]], w_recv.at[slot], peer)
        counter[0] += 1
        copy.start()
        sends.append((None, copy))

    def w_wait(slot):
        remote(wbuf.at[slot], wbuf.at[slot], w_send.at[0], w_recv.at[slot], at(y, t, ob)).wait_recv()

    if n > 2:
        for side in (right, left):
            w_put(columns(b), me_slot, at(y, side, b))
            w_put(columns(ob), me_slot, at(y, side, ob))
    arrived = []

    def forward(s):
        last = n // 2
        from_left, from_right = chip(pos - s), chip(pos + s)
        jobs = []
        if s < last:
            for beta in range(2):
                jobs += [(beta * n + from_left, right, s < last - 1 or beta == 0),
                         (beta * n + from_right, left, s < last - 1 or beta == 1)]
        else:
            jobs = [(from_left, right, False), (n + from_right, left, False)]
        for slot, side, on in jobs:
            w_wait(slot)
            if on:
                w_put(wbuf.at[slot], slot, at(y, side, b))
            arrived.append(slot)

    def pack(x):
        hi = x[HD:].astype(bf16).astype(f32)
        return jnp.concatenate([x[:HD], hi, x[HD:] - hi], axis=0).astype(bf16)

    def unpack(x):
        x = x.astype(f32)
        return jnp.concatenate([x[:HD], x[HD : HD + 8] + x[HD + 8 :]], axis=0)

    state[...] = jnp.zeros_like(state)
    ones = jnp.ones((8, tokens), bf16)
    for g in range(groups):
        lo, wide = g * LANES, min(LANES, depth - g * LANES)
        kg = jnp.maximum(k_ref[:, lo : lo + wide], 0)
        vg = v_ref[:, lo : lo + wide]
        full = lax.dot_general(kg, vg, (((0,), (0,)), ((), ())), preferred_element_type=f32)
        head = lax.broadcasted_iota(jnp.int32, (HD, wide), 1) // HD
        small = full[:HD]
        for h in range(1, wide // HD):
            small = jnp.where(head == h, full[h * HD : (h + 1) * HD], small)
        sums = jnp.dot(ones, kg, preferred_element_type=f32)
        where = pl.ds((g % per_half) * LANES, wide)
        state[g // per_half, :HD, where] = small
        state[g // per_half, HD:, where] = sums

    band_out[...] = pack(state[ob])
    swap = remote(band_out, band_in, s_send.at[0], s_recv.at[0], at(y, t, ob))
    swap.start()
    sends.append((None, swap))
    swap.wait_recv()
    own[...] = state[b] + unpack(band_in[...])

    for s in range(hops):
        d = 1 << s
        hop = remote(
            hop_out.at[s], hop_in.at[s], s_send.at[1 + s], s_recv.at[1 + s],
            at(y, lax.rem(t + d, n), b),
        )
        hop_out[s] = pack(own[...])

        @pl.when(t + d < n)
        def _():
            hop.start()

        sends.append((t + d < n, hop))

        @pl.when(t >= d)
        def _():
            hop.wait_recv()
            own[...] += unpack(hop_in[s])

    final[b] = pack(own[...])
    swap = remote(final.at[b], final.at[b], s_send.at[1 + hops], s_recv.at[1 + hops], at(y, t, ob))
    swap.start()
    sends.append((None, swap))
    if n > 2:
        forward(1)
    swap.wait_recv()

    total = jnp.zeros((tokens, 1), f32)
    for g in range(groups):
        lo, wide = g * LANES, min(LANES, depth - g * LANES)
        qg = jnp.maximum(q_ref[:, lo : lo + wide], 0)
        packed = final[g // per_half, :, pl.ds((g % per_half) * LANES, wide)]
        same = (
            lax.broadcasted_iota(jnp.int32, (wide, wide), 0) // HD
            == lax.broadcasted_iota(jnp.int32, (wide, wide), 1) // HD
        )
        small = packed.astype(f32)
        tall = jnp.concatenate([small[:HD]] * (wide // HD), axis=0)
        numer = jnp.dot(qg, jnp.where(same, tall, 0.0).astype(bf16), preferred_element_type=f32)
        weigh = small[HD : HD + 1] + small[HD + 8 : HD + 9]
        terms = qg.astype(f32) * weigh
        hi = terms.astype(bf16)
        rest = (terms - hi.astype(f32)).astype(bf16)
        block_ones = jnp.where(same, 1.0, 0.0).astype(bf16)
        denom = (
            jnp.dot(hi, block_ones, preferred_element_type=f32)
            + jnp.dot(rest, block_ones, preferred_element_type=f32)
        )
        r = numer / (denom + read_epsilon)
        reads[:, lo : lo + wide] = r
        total = total + jnp.sum(r * r, axis=-1, keepdims=True)
    scale = lax.rsqrt(total * (1.0 / depth) + norm_epsilon)
    abuf[mine] = (reads[...] * scale * g_ref[...]).astype(bf16)

    partner_slot, far_slot, far_partner = y * 2 + ob, oy * 2 + b, oy * 2 + ob

    def a_put(slot, i, peer):
        copy = remote(abuf.at[slot], abuf.at[slot], a_send.at[i], a_recv.at[slot], peer)
        copy.start()
        sends.append((None, copy))

    def a_wait(slot):
        remote(abuf.at[slot], abuf.at[slot], a_send.at[0], a_recv.at[slot], at(y, t, ob)).wait_recv()

    a_put(mine, 0, at(oy, t, b))
    a_put(mine, 1, at(y, t, ob))

    shards = 2 * n
    acut[...] = jnp.zeros_like(acut)

    def cut(slot):
        for j in range(shards):
            acut[j, slot, :, :shard_rows] = abuf[slot, :, j * shard_rows : (j + 1) * shard_rows]

    cut(mine)
    if n > 4:
        forward(2)
    a_wait(partner_slot)
    cut(partner_slot)
    a_wait(far_slot)
    a_put(far_slot, 2, at(y, t, ob))
    cut(far_slot)
    for s in range(3, n // 2):
        forward(s)
    a_wait(far_partner)
    cut(far_partner)
    local.wait()
    partner_rows = ob * n + t
    w_wait(partner_rows)

    acc[...] = jnp.zeros_like(acc)

    def add(slot):
        acc[...] += jnp.dot(
            acut[slot].reshape(4 * tokens, acut.shape[3]), wbuf[slot], preferred_element_type=f32
        )

    add(me_slot)
    add(partner_rows)
    for slot in list(arrived):
        add(slot)
    arrived.clear()
    forward(n // 2)
    for slot in arrived:
        add(slot)

    def rows_of(slot):
        return acc[pl.ds(pl.multiple_of(slot * tokens, 8), tokens), :].astype(bf16)

    for i, (slot, peer) in enumerate(
        [(far_slot, at(oy, t, b)), (far_partner, at(oy, t, ob)), (partner_slot, at(y, t, ob))]
    ):
        res_out[i] = rows_of(slot)
        copy = remote(res_out.at[i], res_in.at[mine], r_send.at[i], r_recv.at[mine], peer)
        copy.start()
        sends.append((None, copy))
    res_in[mine] = rows_of(mine)
    for slot in (partner_slot, far_slot, far_partner):
        remote(
            res_in.at[slot], res_in.at[slot], r_send.at[0], r_recv.at[slot], at(y, t, ob)
        ).wait_recv()
    for c in range(4):
        wide = min(block, depth - c * block)
        out_ref[:, c * block : c * block + wide] = res_in[c, :, :wide]
    for condition, copy in sends:
        if condition is None:
            copy.wait_send()
        else:
            pl.when(condition)(copy.wait_send)


def fast_body(n, query_tokens, key_tokens, value_tokens, norm_gain, out_weight):
    frames, rows, width, depth = query_tokens.shape
    tokens = frames * rows * width
    shard_rows = out_weight.size // depth
    padded = round_up(shard_rows, 16)
    block = round_up(-(-depth // 4), LANES)
    half = round_up(-(-depth // 2), LANES)
    hops = n.bit_length() - 1
    weight = jnp.pad(
        out_weight.reshape(shard_rows, depth),
        ((0, padded - shard_rows), (0, 4 * block - depth)),
    )
    flat = [x.reshape(tokens, depth) for x in (query_tokens, key_tokens, value_tokens)]
    f32, bf16 = jnp.float32, jnp.bfloat16
    packed = HD + 16
    dma = pltpu.SemaphoreType.DMA
    out = pl.pallas_call(
        functools.partial(kernel, n, shard_rows),
        out_shape=jax.ShapeDtypeStruct((tokens, depth), bf16),
        in_specs=[pl.BlockSpec(memory_space=pltpu.VMEM)] * 5,
        out_specs=pl.BlockSpec(memory_space=pltpu.VMEM),
        scratch_shapes=[
            pltpu.VMEM((2, HD + 8, half), f32),
            pltpu.VMEM((HD + 8, half), f32),
            pltpu.VMEM((packed, half), bf16),
            pltpu.VMEM((packed, half), bf16),
            pltpu.VMEM((hops, packed, half), bf16),
            pltpu.VMEM((hops, packed, half), bf16),
            pltpu.VMEM((2, packed, half), bf16),
            pltpu.VMEM((tokens, depth), f32),
            pltpu.VMEM((2 * n, padded, block), bf16),
            pltpu.VMEM((4, tokens, depth), bf16),
            pltpu.VMEM((2 * n, 4, tokens, padded), bf16),
            pltpu.VMEM((4 * tokens, block), f32),
            pltpu.VMEM((3, tokens, block), bf16),
            pltpu.VMEM((4, tokens, block), bf16),
            dma(()),
            dma((2 * n + 8,)),
            dma((2 * n,)),
            dma((hops + 2,)),
            dma((hops + 2,)),
            dma((3,)),
            dma((4,)),
            dma((3,)),
            dma((4,)),
        ],
        compiler_params=pltpu.CompilerParams(
            collective_id=0, has_side_effects=True, vmem_limit_bytes=48 * 1024 * 1024
        ),
    )(*flat, norm_gain.reshape(1, depth), weight)
    return out.reshape(query_tokens.shape)


def solution(mesh):
    n, bands, parts = mesh.shape["tm"], mesh.shape["band"], mesh.shape["parts"]

    def body(query_tokens, key_tokens, value_tokens, norm_gain, out_weight):
        depth = query_tokens.shape[3]
        ring = n >= 4 and n & (n - 1) == 0 and bands == 2 and parts == 2
        if ring and query_tokens.shape[0] == 1 and out_weight.size % depth == 0:
            return fast_body(n, query_tokens, key_tokens, value_tokens, norm_gain, out_weight)
        return plain_body(query_tokens, key_tokens, value_tokens, norm_gain, out_weight)

    spread = P(("parts", "tm"), "band", None, None)
    return jax.shard_map(
        body,
        mesh=mesh,
        in_specs=(spread, spread, spread, P(), P("band", "tm", None)),
        out_specs=spread,
        check_vma=False,
    )
```

```python
import functools

import jax
import jax.numpy as jnp
from jax import lax
from jax.experimental import pallas as pl
from jax.experimental.pallas import tpu as pltpu
from jax.sharding import PartitionSpec as P

HEADS = 70
HD = 32
LANES = 128

norm_epsilon = 1e-06
read_epsilon = 1e-06
MESH = pl.DeviceIdType.MESH


def round_up(x, m):
    return -(-x // m) * m


def entering(x, axis):
    peers, place = (lax.axis_size(axis), lax.axis_index(axis))
    everything = jax.tree.map(lambda part: lax.all_gather(part, axis), x)

    def hop(k, before):
        return jax.tree.map(
            lambda a, part: jnp.where(k < place, a + part[k], a), before, everything
        )

    return lax.fori_loop(0, peers, hop, jax.tree.map(jnp.zeros_like, x))


def plain_body(query_tokens, key_tokens, value_tokens, norm_gain, out_weight):
    frames, rows, width, depth = query_tokens.shape
    key_relu = jax.nn.relu(key_tokens).reshape(frames, rows * width, HEADS, HD)
    value_heads = value_tokens.reshape(frames, rows * width, HEADS, HD)
    part_state = jnp.einsum(
        "fthd,fthe->fhde", key_relu, value_heads, preferred_element_type=jnp.float32
    ).reshape(frames, HEADS, HD * HD)
    part_norm = jnp.sum(key_relu, axis=1, dtype=jnp.float32)
    state_sum, norm_sum = lax.psum((part_state, part_norm), "band")
    local_state = jnp.cumsum(state_sum, axis=0)
    local_norm = jnp.cumsum(norm_sum, axis=0)
    before = entering((local_state[-1], local_norm[-1]), "tm")
    prefix_state = local_state + before[0]
    prefix_norm = local_norm + before[1]
    query_relu = jax.nn.relu(query_tokens.astype(jnp.float32)).reshape(
        frames, rows * width, HEADS, HD
    )
    numer = jnp.einsum(
        "fthd,fhde->fthe",
        query_relu,
        prefix_state.reshape(frames, HEADS, HD, HD),
        precision=lax.Precision.HIGHEST,
    )
    denom = (
        jnp.einsum("fthd,fhd->fth", query_relu, prefix_norm, precision=lax.Precision.HIGHEST)
        + read_epsilon
    )
    reads = (numer / denom[:, :, :, None]).reshape(frames * rows * width, depth)
    square = jnp.mean(reads * reads, axis=-1, keepdims=True)
    normed = (reads * lax.rsqrt(square + norm_epsilon) * norm_gain).astype(jnp.bfloat16)
    gathered = lax.all_gather(out_weight, "tm", axis=1, tiled=True)
    rows_half = gathered.reshape(-1, depth)
    result = jnp.dot(
        normed,
        lax.all_gather(rows_half, "band", axis=0, tiled=True),
        preferred_element_type=jnp.float32,
    )
    return result.astype(jnp.bfloat16).reshape(frames, rows, width, depth)


def kernel(
    n, shard_rows,
    q_ref, k_ref, v_ref, g_ref, chunks_ref, out_ref,
    w_wide, w_ref, state, own, band_out, band_in, hop_out, hop_in, final, reads,
    wbuf, abuf, acut, acc, res_out, res_in,
    w_local_sem, w_send, w_recv, s_send, s_recv, a_send, a_recv, r_send, r_recv,
):
    f32, bf16 = jnp.float32, jnp.bfloat16
    tokens, depth = q_ref.shape
    half = state.shape[2] - LANES
    block = wbuf.shape[2]
    hops = n.bit_length() - 1
    groups = -(-depth // LANES)
    per_half = half // LANES

    y, t, b = lax.axis_index("parts"), lax.axis_index("tm"), lax.axis_index("band")
    oy, ob = 1 - y, 1 - b
    mine = y * 2 + b

    def at(py, pt, pb):
        return {"parts": py, "tm": pt, "band": pb}

    odd = t % 2
    pos = (1 - odd) * (t // 2) + odd * (n - 1 - t // 2)

    def chip(p):
        p = lax.rem(p + 2 * n, n)
        back = p // (n // 2)
        return (1 - back) * (2 * p) + back * (2 * (n - 1 - p) + 1)

    right, left = chip(pos + 1), chip(pos - 1)

    barrier = pltpu.get_barrier_semaphore()
    peers = [at(y, t, ob), at(oy, t, b), at(oy, t, ob)]
    for side in (right, left):
        peers += [at(y, side, b), at(y, side, ob)]
    for s in range(hops):
        d = 1 << s
        peers += [at(y, lax.rem(t + d, n), b), at(y, lax.rem(t + n - d, n), b)]
    for peer in peers:
        pl.semaphore_signal(barrier, inc=1, device_id=peer, device_id_type=MESH)

    pairs, per_pair, tiles = shard_rows // 2, 2 * depth // LANES, -(-depth // LANES)
    w_wide[...] = jnp.zeros_like(w_wide)
    lower = lax.broadcasted_iota(jnp.int32, (pairs, LANES), 1) < LANES // 2

    def chunk(j):
        return chunks_ref[pl.ds(j, pairs, stride=per_pair), :]

    middle = chunk(tiles - 1)
    for j in range(tiles - 1):
        w_wide[j, pl.ds(0, pairs, stride=2), :] = chunk(j)
    w_wide[tiles - 1, pl.ds(0, pairs, stride=2), :] = jnp.where(lower, middle, 0.0)
    turned = pltpu.roll(middle, LANES // 2, 1)
    for j in range(tiles):
        if j + 1 < tiles:
            following = pltpu.roll(chunk(tiles + j), LANES // 2, 1)
        else:
            following = jnp.zeros_like(turned)
        w_wide[j, pl.ds(1, pairs, stride=2), :] = jnp.where(lower, turned, following)
        turned = following
    for j in range(w_wide.shape[0]):
        w_ref[:, j * LANES : (j + 1) * LANES] = w_wide[j].astype(bf16)
    pl.semaphore_wait(barrier, len(peers))

    def remote(src, dst, send, recv, peer):
        return pltpu.make_async_remote_copy(
            src_ref=src, dst_ref=dst, send_sem=send, recv_sem=recv,
            device_id=peer, device_id_type=MESH,
        )

    def columns(pb):
        return w_ref.at[:, pl.ds(pl.multiple_of((y * 2 + pb) * block, LANES), block)]

    sends = []
    me_slot = b * n + t
    local = pltpu.make_async_copy(columns(b), wbuf.at[me_slot], w_local_sem)
    local.start()
    pair = remote(columns(ob), wbuf.at[me_slot], w_send.at[0], w_recv.at[me_slot], at(y, t, ob))
    pair.start()
    sends.append((None, pair))
    counter = [1]

    def w_put(src, slot, peer):
        copy = remote(src, wbuf.at[slot], w_send.at[counter[0]], w_recv.at[slot], peer)
        counter[0] += 1
        copy.start()
        sends.append((None, copy))

    def w_wait(slot):
        remote(wbuf.at[slot], wbuf.at[slot], w_send.at[0], w_recv.at[slot], at(y, t, ob)).wait_recv()

    if n > 2:
        for side in (right, left):
            w_put(columns(b), me_slot, at(y, side, b))
            w_put(columns(ob), me_slot, at(y, side, ob))
    arrived = []

    def forward(s):
        last = n // 2
        from_left, from_right = chip(pos - s), chip(pos + s)
        jobs = []
        if s < last:
            for beta in range(2):
                jobs += [(beta * n + from_left, right, s < last - 1 or beta == 0),
                         (beta * n + from_right, left, s < last - 1 or beta == 1)]
        else:
            jobs = [(from_left, right, False), (n + from_right, left, False)]
        for slot, side, on in jobs:
            w_wait(slot)
            if on:
                w_put(wbuf.at[slot], slot, at(y, side, b))
            arrived.append(slot)

    rows = HD // 2

    def pack(x):
        sums = x[:rows, half:]
        hi = sums.astype(bf16).astype(f32)
        both = jnp.concatenate([hi, sums - hi], axis=0)
        return jnp.concatenate([x[:, :half], both], axis=1).astype(bf16)

    def unpack(x):
        x = x.astype(f32)
        sums = x[:rows, half:] + x[rows:, half:]
        sums = jnp.concatenate([sums, jnp.zeros_like(sums)], axis=0)
        return jnp.concatenate([x[:, :half], sums], axis=1)

    state[...] = jnp.zeros_like(state)
    ones = jnp.ones((8, tokens), bf16)
    for g in range(groups):
        lo, wide = g * LANES, min(LANES, depth - g * LANES)
        kg = jnp.maximum(k_ref[:, lo : lo + wide], 0)
        vg = v_ref[:, lo : lo + wide]
        full = lax.dot_general(kg, vg, (((0,), (0,)), ((), ())), preferred_element_type=f32)
        head = lax.broadcasted_iota(jnp.int32, (HD, wide), 1) // HD
        small = full[:HD]
        for h in range(1, wide // HD):
            small = jnp.where(head == h, full[h * HD : (h + 1) * HD], small)
        sums = jnp.dot(ones, kg, preferred_element_type=f32)
        where = pl.ds((g % per_half) * LANES, wide)
        state[g // per_half, :, where] = small
        row = g % per_half
        state[g // per_half, row : row + 1, half : half + wide] = sums[:1]

    band_out[...] = pack(state[ob])
    swap = remote(band_out, band_in, s_send.at[0], s_recv.at[0], at(y, t, ob))
    swap.start()
    sends.append((None, swap))
    swap.wait_recv()
    own[...] = state[b] + unpack(band_in[...])

    for s in range(hops):
        d = 1 << s
        hop = remote(
            hop_out.at[s], hop_in.at[s], s_send.at[1 + s], s_recv.at[1 + s],
            at(y, lax.rem(t + d, n), b),
        )
        hop_out[s] = pack(own[...])

        @pl.when(t + d < n)
        def _():
            hop.start()

        sends.append((t + d < n, hop))
        if s == hops - 1:
            forward(1)

        @pl.when(t >= d)
        def _():
            hop.wait_recv()
            own[...] += unpack(hop_in[s])

    final[b] = pack(own[...])
    swap = remote(final.at[b], final.at[b], s_send.at[1 + hops], s_recv.at[1 + hops], at(y, t, ob))
    swap.start()
    sends.append((None, swap))
    swap.wait_recv()

    total = jnp.zeros((tokens, 1), f32)
    for g in range(groups):
        lo, wide = g * LANES, min(LANES, depth - g * LANES)
        qg = jnp.maximum(q_ref[:, lo : lo + wide], 0)
        packed = final[g // per_half, :, pl.ds((g % per_half) * LANES, wide)]
        same = (
            lax.broadcasted_iota(jnp.int32, (wide, wide), 0) // HD
            == lax.broadcasted_iota(jnp.int32, (wide, wide), 1) // HD
        )
        small = packed.astype(f32)
        tall = jnp.concatenate([small] * (wide // HD), axis=0)
        numer = jnp.dot(qg, jnp.where(same, tall, 0.0).astype(bf16), preferred_element_type=f32)
        sums = final[g // per_half, :, half : half + wide].astype(f32)
        row = g % per_half
        weigh = sums[row : row + 1] + sums[rows + row : rows + row + 1]
        terms = qg.astype(f32) * weigh
        hi = terms.astype(bf16)
        rest = (terms - hi.astype(f32)).astype(bf16)
        block_ones = jnp.where(same, 1.0, 0.0).astype(bf16)
        denom = (
            jnp.dot(hi, block_ones, preferred_element_type=f32)
            + jnp.dot(rest, block_ones, preferred_element_type=f32)
        )
        r = numer / (denom + read_epsilon)
        reads[:, lo : lo + wide] = r
        total = total + jnp.sum(r * r, axis=-1, keepdims=True)
    scale = lax.rsqrt(total * (1.0 / depth) + norm_epsilon)
    abuf[mine] = (reads[...] * scale * g_ref[...]).astype(bf16)

    partner_slot, far_slot, far_partner = y * 2 + ob, oy * 2 + b, oy * 2 + ob

    def a_put(slot, i, peer):
        copy = remote(abuf.at[slot], abuf.at[slot], a_send.at[i], a_recv.at[slot], peer)
        copy.start()
        sends.append((None, copy))

    def a_wait(slot):
        remote(abuf.at[slot], abuf.at[slot], a_send.at[0], a_recv.at[slot], at(y, t, ob)).wait_recv()

    a_put(mine, 0, at(oy, t, b))
    a_put(mine, 1, at(y, t, ob))

    shards = 2 * n
    acut[...] = jnp.zeros_like(acut)

    def cut(slot):
        for j in range(shards):
            acut[j, slot, :, :shard_rows] = abuf[slot, :, j * shard_rows : (j + 1) * shard_rows]

    if n > 4:
        forward(2)
    cut(mine)
    a_wait(partner_slot)
    cut(partner_slot)
    for s in range(3, n // 2):
        forward(s)
    local.wait()
    partner_rows = ob * n + t
    w_wait(partner_rows)
    arrived += [me_slot, partner_rows]
    acc[...] = jnp.zeros_like(acc)

    def add(slot, side):
        both = acut[slot, pl.ds(2 * side, 2)].reshape(2 * tokens, acut.shape[3])
        acc[side] += jnp.dot(both, wbuf[slot], preferred_element_type=f32)

    for slot in arrived:
        add(slot, y)
    a_wait(far_slot)
    a_put(far_slot, 2, at(y, t, ob))
    cut(far_slot)
    a_wait(far_partner)
    cut(far_partner)
    for slot in arrived:
        add(slot, oy)
    arrived.clear()
    forward(n // 2)

    def rows_of(side, pb):
        return acc[side, pl.ds(pl.multiple_of(pb * tokens, 8), tokens), :].astype(bf16)

    def give(i, side, pb):
        res_out[i] = rows_of(side, pb)
        copy = remote(
            res_out.at[i], res_in.at[mine], r_send.at[i], r_recv.at[mine], at(side, t, pb)
        )
        copy.start()
        sends.append((None, copy))

    for slot in arrived:
        add(slot, oy)
    give(0, oy, b)
    give(1, oy, ob)
    for slot in arrived:
        add(slot, y)
    give(2, y, ob)
    res_in[mine] = rows_of(y, b)
    for slot in (partner_slot, far_slot, far_partner):
        remote(
            res_in.at[slot], res_in.at[slot], r_send.at[0], r_recv.at[slot], at(y, t, ob)
        ).wait_recv()
    for c in range(4):
        wide = min(block, depth - c * block)
        out_ref[:, c * block : c * block + wide] = res_in[c, :, :wide]
    for condition, copy in sends:
        if condition is None:
            copy.wait_send()
        else:
            pl.when(condition)(copy.wait_send)


def fast_body(n, query_tokens, key_tokens, value_tokens, norm_gain, out_weight):
    frames, rows, width, depth = query_tokens.shape
    tokens = frames * rows * width
    shard_rows = out_weight.size // depth
    padded = round_up(shard_rows, 16)
    block = round_up(-(-depth // 4), LANES)
    half = round_up(-(-depth // 2), LANES)
    hops = n.bit_length() - 1
    weight = out_weight.astype(jnp.float32).reshape(-1, LANES)
    flat = [x.reshape(tokens, depth) for x in (query_tokens, key_tokens, value_tokens)]
    f32, bf16 = jnp.float32, jnp.bfloat16
    packed = half + LANES
    dma = pltpu.SemaphoreType.DMA
    out = pl.pallas_call(
        functools.partial(kernel, n, shard_rows),
        out_shape=jax.ShapeDtypeStruct((tokens, depth), bf16),
        in_specs=[pl.BlockSpec(memory_space=pltpu.VMEM)] * 5,
        out_specs=pl.BlockSpec(memory_space=pltpu.VMEM),
        scratch_shapes=[
            pltpu.VMEM((4 * block // LANES, padded, LANES), f32),
            pltpu.VMEM((padded, 4 * block), bf16),
            pltpu.VMEM((2, HD, packed), f32),
            pltpu.VMEM((HD, packed), f32),
            pltpu.VMEM((HD, packed), bf16),
            pltpu.VMEM((HD, packed), bf16),
            pltpu.VMEM((hops, HD, packed), bf16),
            pltpu.VMEM((hops, HD, packed), bf16),
            pltpu.VMEM((2, HD, packed), bf16),
            pltpu.VMEM((tokens, depth), f32),
            pltpu.VMEM((2 * n, padded, block), bf16),
            pltpu.VMEM((4, tokens, depth), bf16),
            pltpu.VMEM((2 * n, 4, tokens, padded), bf16),
            pltpu.VMEM((2, 2 * tokens, block), f32),
            pltpu.VMEM((3, tokens, block), bf16),
            pltpu.VMEM((4, tokens, block), bf16),
            dma(()),
            dma((2 * n + 8,)),
            dma((2 * n,)),
            dma((hops + 2,)),
            dma((hops + 2,)),
            dma((3,)),
            dma((4,)),
            dma((3,)),
            dma((4,)),
        ],
        compiler_params=pltpu.CompilerParams(
            collective_id=0, has_side_effects=True, vmem_limit_bytes=48 * 1024 * 1024
        ),
    )(*flat, norm_gain.reshape(1, depth), weight)
    return out.reshape(query_tokens.shape)


def solution(mesh):
    n, bands, parts = mesh.shape["tm"], mesh.shape["band"], mesh.shape["parts"]

    def body(query_tokens, key_tokens, value_tokens, norm_gain, out_weight):
        depth = query_tokens.shape[3]
        ring = n >= 4 and n & (n - 1) == 0 and bands == 2 and parts == 2
        whole_pairs = out_weight.size % (2 * depth) == 0 and depth % LANES == LANES // 2
        few = round_up(-(-depth // 2), LANES) // LANES <= HD // 2
        if ring and query_tokens.shape[0] == 1 and whole_pairs and few:
            return fast_body(n, query_tokens, key_tokens, value_tokens, norm_gain, out_weight)
        return plain_body(query_tokens, key_tokens, value_tokens, norm_gain, out_weight)

    spread = P(("parts", "tm"), "band", None, None)
    return jax.shard_map(
        body,
        mesh=mesh,
        in_specs=(spread, spread, spread, P(), P("band", "tm", None)),
        out_specs=spread,
        check_vma=False,
    )
```

```python
import functools

import jax
import jax.numpy as jnp
from jax import lax
from jax.experimental import pallas as pl
from jax.experimental.pallas import tpu as pltpu
from jax.sharding import PartitionSpec as P

HEADS = 70
HD = 32
LANES = 128

norm_epsilon = 1e-06
read_epsilon = 1e-06
MESH = pl.DeviceIdType.MESH


def round_up(x, m):
    return -(-x // m) * m


def entering(x, axis):
    peers, place = (lax.axis_size(axis), lax.axis_index(axis))
    everything = jax.tree.map(lambda part: lax.all_gather(part, axis), x)

    def hop(k, before):
        return jax.tree.map(
            lambda a, part: jnp.where(k < place, a + part[k], a), before, everything
        )

    return lax.fori_loop(0, peers, hop, jax.tree.map(jnp.zeros_like, x))


def plain_body(query_tokens, key_tokens, value_tokens, norm_gain, out_weight):
    frames, rows, width, depth = query_tokens.shape
    key_relu = jax.nn.relu(key_tokens).reshape(frames, rows * width, HEADS, HD)
    value_heads = value_tokens.reshape(frames, rows * width, HEADS, HD)
    part_state = jnp.einsum(
        "fthd,fthe->fhde", key_relu, value_heads, preferred_element_type=jnp.float32
    ).reshape(frames, HEADS, HD * HD)
    part_norm = jnp.sum(key_relu, axis=1, dtype=jnp.float32)
    state_sum, norm_sum = lax.psum((part_state, part_norm), "band")
    local_state = jnp.cumsum(state_sum, axis=0)
    local_norm = jnp.cumsum(norm_sum, axis=0)
    before = entering((local_state[-1], local_norm[-1]), "tm")
    prefix_state = local_state + before[0]
    prefix_norm = local_norm + before[1]
    query_relu = jax.nn.relu(query_tokens.astype(jnp.float32)).reshape(
        frames, rows * width, HEADS, HD
    )
    numer = jnp.einsum(
        "fthd,fhde->fthe",
        query_relu,
        prefix_state.reshape(frames, HEADS, HD, HD),
        precision=lax.Precision.HIGHEST,
    )
    denom = (
        jnp.einsum("fthd,fhd->fth", query_relu, prefix_norm, precision=lax.Precision.HIGHEST)
        + read_epsilon
    )
    reads = (numer / denom[:, :, :, None]).reshape(frames * rows * width, depth)
    square = jnp.mean(reads * reads, axis=-1, keepdims=True)
    normed = (reads * lax.rsqrt(square + norm_epsilon) * norm_gain).astype(jnp.bfloat16)
    gathered = lax.all_gather(out_weight, "tm", axis=1, tiled=True)
    rows_half = gathered.reshape(-1, depth)
    result = jnp.dot(
        normed,
        lax.all_gather(rows_half, "band", axis=0, tiled=True),
        preferred_element_type=jnp.float32,
    )
    return result.astype(jnp.bfloat16).reshape(frames, rows, width, depth)


def kernel(
    n, shard_rows,
    q_ref, k_ref, v_ref, g_ref, flat_ref, out_ref,
    chunks_ref, w_wide, w_ref, state, own, band_out, band_in, hop_out, hop_in, final, reads,
    wbuf, wrest, abuf, acc, res_out, res_in,
    w_local_sem, w_send, w_recv, e_send, e_recv, s_send, s_recv, a_send, a_recv, r_send, r_recv,
):
    f32, bf16 = jnp.float32, jnp.bfloat16
    tokens, depth = q_ref.shape
    half = state.shape[2] - LANES
    block = wbuf.shape[2]
    hops = n.bit_length() - 1
    groups = -(-depth // LANES)
    per_half = half // LANES

    y, t, b = lax.axis_index("parts"), lax.axis_index("tm"), lax.axis_index("band")
    oy, ob = 1 - y, 1 - b
    mine = y * 2 + b

    def at(py, pt, pb):
        return {"parts": py, "tm": pt, "band": pb}

    odd = t % 2
    pos = (1 - odd) * (t // 2) + odd * (n - 1 - t // 2)

    def chip(p):
        p = lax.rem(p + 2 * n, n)
        back = p // (n // 2)
        return (1 - back) * (2 * p) + back * (2 * (n - 1 - p) + 1)

    right, left = chip(pos + 1), chip(pos - 1)

    barrier = pltpu.get_barrier_semaphore()
    peers = [at(y, t, ob), at(oy, t, b), at(oy, t, ob)]
    for side in (right, left):
        peers += [at(y, side, b), at(y, side, ob)]
    for s in range(hops):
        d = 1 << s
        peers += [at(y, lax.rem(t + d, n), b), at(y, lax.rem(t + n - d, n), b)]
    for peer in peers:
        pl.semaphore_signal(barrier, inc=1, device_id=peer, device_id_type=MESH)

    size = flat_ref.shape[2]
    for lo in range(0, size, 8 * LANES):
        wide = min(8 * LANES, size - lo)
        chunks_ref[lo // LANES : (lo + wide) // LANES, :] = (
            flat_ref[0, :, lo : lo + wide].astype(f32).reshape(wide // LANES, LANES)
        )
    pairs, per_pair, tiles = shard_rows // 2, 2 * depth // LANES, -(-depth // LANES)
    w_wide[...] = jnp.zeros_like(w_wide)
    lower = lax.broadcasted_iota(jnp.int32, (pairs, LANES), 1) < LANES // 2

    def chunk(j):
        return chunks_ref[pl.ds(j, pairs, stride=per_pair), :]

    middle = chunk(tiles - 1)
    for j in range(tiles - 1):
        w_wide[j, pl.ds(0, pairs, stride=2), :] = chunk(j)
    w_wide[tiles - 1, pl.ds(0, pairs, stride=2), :] = jnp.where(lower, middle, 0.0)
    turned = pltpu.roll(middle, LANES // 2, 1)
    for j in range(tiles):
        if j + 1 < tiles:
            following = pltpu.roll(chunk(tiles + j), LANES // 2, 1)
        else:
            following = jnp.zeros_like(turned)
        w_wide[j, pl.ds(1, pairs, stride=2), :] = jnp.where(lower, turned, following)
        turned = following
    for j in range(w_wide.shape[0]):
        w_ref[:, j * LANES : (j + 1) * LANES] = w_wide[j].astype(bf16)
    pl.semaphore_wait(barrier, len(peers))

    def remote(src, dst, send, recv, peer):
        return pltpu.make_async_remote_copy(
            src_ref=src, dst_ref=dst, send_sem=send, recv_sem=recv,
            device_id=peer, device_id_type=MESH,
        )

    main = wbuf.shape[1]
    sends = []
    counter = [0]

    def columns(pb, lo, size):
        return w_ref.at[pl.ds(lo, size), pl.ds(pl.multiple_of((y * 2 + pb) * block, LANES), block)]

    def w_put(sources, slot, peer):
        i = counter[0]
        counter[0] += 1
        for src, buf, sent, got in zip(sources, (wbuf, wrest), (w_send, e_send), (w_recv, e_recv)):
            copy = remote(src, buf.at[slot], sent.at[i], got.at[slot], peer)
            copy.start()
            sends.append((None, copy))

    def w_wait(slot):
        for buf, sent, got in ((wbuf, w_send, w_recv), (wrest, e_send, e_recv)):
            remote(buf.at[slot], buf.at[slot], sent.at[0], got.at[slot], at(y, t, ob)).wait_recv()

    me_slot = 2 * t + b
    own_rows = [(columns(pb, 0, main), columns(pb, main, wrest.shape[1])) for pb in (b, ob)]
    for side in (right, left):
        w_put(own_rows[0], me_slot, at(y, side, b))
        w_put(own_rows[1], me_slot, at(y, side, ob))
    w_put(own_rows[1], me_slot, at(y, t, ob))
    locals_ = [
        pltpu.make_async_copy(src, buf.at[me_slot], w_local_sem.at[i])
        for i, (src, buf) in enumerate(zip(own_rows[0], (wbuf, wrest)))
    ]
    for copy in locals_:
        copy.start()
    arrived = []

    def forward(s):
        last = n // 2
        from_left, from_right = chip(pos - s), chip(pos + s)
        jobs = []
        if s < last:
            for beta in range(2):
                jobs += [(2 * from_left + beta, right, s < last - 1 or beta == 0),
                         (2 * from_right + beta, left, s < last - 1 or beta == 1)]
            arrived.extend([from_left, from_right])
        else:
            jobs = [(2 * from_left, right, False), (2 * from_right + 1, left, False)]
            arrived.append(from_left)
        for slot, side, on in jobs:
            w_wait(slot)
            if on:
                w_put((wbuf.at[slot], wrest.at[slot]), slot, at(y, side, b))

    rows = HD // 2

    def pack(x):
        sums = x[:rows, half:]
        hi = sums.astype(bf16).astype(f32)
        both = jnp.concatenate([hi, sums - hi], axis=0)
        return jnp.concatenate([x[:, :half], both], axis=1).astype(bf16)

    def unpack(x):
        x = x.astype(f32)
        sums = x[:rows, half:] + x[rows:, half:]
        sums = jnp.concatenate([sums, jnp.zeros_like(sums)], axis=0)
        return jnp.concatenate([x[:, :half], sums], axis=1)

    state[...] = jnp.zeros_like(state)
    ones = jnp.ones((8, tokens), bf16)
    for g in range(groups):
        lo, wide = g * LANES, min(LANES, depth - g * LANES)
        kg = jnp.maximum(k_ref[:, lo : lo + wide], 0)
        vg = v_ref[:, lo : lo + wide]
        full = lax.dot_general(kg, vg, (((0,), (0,)), ((), ())), preferred_element_type=f32)
        head = lax.broadcasted_iota(jnp.int32, (HD, wide), 1) // HD
        small = full[:HD]
        for h in range(1, wide // HD):
            small = jnp.where(head == h, full[h * HD : (h + 1) * HD], small)
        sums = jnp.dot(ones, kg, preferred_element_type=f32)
        where = pl.ds((g % per_half) * LANES, wide)
        state[g // per_half, :, where] = small
        row = g % per_half
        state[g // per_half, row : row + 1, half : half + wide] = sums[:1]

    band_out[...] = pack(state[ob])
    swap = remote(band_out, band_in, s_send.at[0], s_recv.at[0], at(y, t, ob))
    swap.start()
    sends.append((None, swap))
    swap.wait_recv()
    own[...] = state[b] + unpack(band_in[...])

    for s in range(hops):
        d = 1 << s
        hop = remote(
            hop_out.at[s], hop_in.at[s], s_send.at[1 + s], s_recv.at[1 + s],
            at(y, lax.rem(t + d, n), b),
        )
        hop_out[s] = pack(own[...])

        @pl.when(t + d < n)
        def _():
            hop.start()

        sends.append((t + d < n, hop))
        if s == hops - 1:
            forward(1)

        @pl.when(t >= d)
        def _():
            hop.wait_recv()
            own[...] += unpack(hop_in[s])

    final[b] = pack(own[...])
    swap = remote(final.at[b], final.at[b], s_send.at[1 + hops], s_recv.at[1 + hops], at(y, t, ob))
    swap.start()
    sends.append((None, swap))
    swap.wait_recv()

    total = jnp.zeros((tokens, 1), f32)
    for g in range(groups):
        lo, wide = g * LANES, min(LANES, depth - g * LANES)
        qg = jnp.maximum(q_ref[:, lo : lo + wide], 0)
        packed = final[g // per_half, :, pl.ds((g % per_half) * LANES, wide)]
        same = (
            lax.broadcasted_iota(jnp.int32, (wide, wide), 0) // HD
            == lax.broadcasted_iota(jnp.int32, (wide, wide), 1) // HD
        )
        small = packed.astype(f32)
        tall = jnp.concatenate([small] * (wide // HD), axis=0)
        numer = jnp.dot(qg, jnp.where(same, tall, 0.0).astype(bf16), preferred_element_type=f32)
        sums = final[g // per_half, :, half : half + wide].astype(f32)
        row = g % per_half
        weigh = sums[row : row + 1] + sums[rows + row : rows + row + 1]
        terms = qg.astype(f32) * weigh
        hi = terms.astype(bf16)
        rest = (terms - hi.astype(f32)).astype(bf16)
        block_ones = jnp.where(same, 1.0, 0.0).astype(bf16)
        denom = (
            jnp.dot(hi, block_ones, preferred_element_type=f32)
            + jnp.dot(rest, block_ones, preferred_element_type=f32)
        )
        r = numer / (denom + read_epsilon)
        reads[:, lo : lo + wide] = r
        total = total + jnp.sum(r * r, axis=-1, keepdims=True)
    scale = lax.rsqrt(total * (1.0 / depth) + norm_epsilon)
    normed = reads[...] * scale * g_ref[...][None, :]
    shards, few = 2 * n, shard_rows - main
    gap = jnp.zeros((tokens, wrest.shape[1] - few), f32)
    extra = []
    for j in range(shards):
        slot, lo = 2 * (j % n) + j // n, j * shard_rows
        abuf[mine, :, slot * main : (slot + 1) * main] = normed[:, lo : lo + main].astype(bf16)
    for slot in range(shards):
        lo = (slot % 2 * n + slot // 2) * shard_rows + main
        extra += [normed[:, lo : lo + few], gap]
    abuf[mine, :, shards * main :] = jnp.concatenate(extra, axis=1).astype(bf16)

    partner_slot, far_slot, far_partner = y * 2 + ob, oy * 2 + b, oy * 2 + ob

    def a_put(slot, i, peer):
        copy = remote(abuf.at[slot], abuf.at[slot], a_send.at[i], a_recv.at[slot], peer)
        copy.start()
        sends.append((None, copy))

    def a_wait(slot):
        remote(abuf.at[slot], abuf.at[slot], a_send.at[0], a_recv.at[slot], at(y, t, ob)).wait_recv()

    a_put(mine, 0, at(oy, t, b))
    a_put(mine, 1, at(y, t, ob))

    if n > 4:
        forward(2)
    acc[...] = jnp.zeros_like(acc)
    a_wait(partner_slot)
    for s in range(3, n // 2):
        forward(s)
    for copy in locals_:
        copy.wait()
    w_wait(2 * t + ob)
    arrived.append(t)

    def add(p, side):
        lanes = pl.ds(pl.multiple_of(p * 2 * main, LANES), 2 * main)
        both = abuf[pl.ds(2 * side, 2), :, lanes].reshape(2 * tokens, 2 * main)
        rows = wbuf[pl.ds(2 * p, 2)].reshape(2 * main, block)
        acc[side] += jnp.dot(both, rows, preferred_element_type=f32)

    def add_rest(side):
        both = abuf[pl.ds(2 * side, 2), :, shards * main :].reshape(2 * tokens, -1)
        rows = wrest[...].reshape(-1, block)
        acc[side] += jnp.dot(both, rows, preferred_element_type=f32)

    for p in arrived:
        add(p, y)
    a_wait(far_slot)
    a_put(far_slot, 2, at(y, t, ob))
    a_wait(far_partner)
    for p in arrived:
        add(p, oy)
    arrived.clear()
    forward(n // 2)

    def rows_of(side, pb):
        return acc[side, pl.ds(pl.multiple_of(pb * tokens, 8), tokens), :].astype(bf16)

    def give(i, side, pb):
        res_out[i] = rows_of(side, pb)
        copy = remote(
            res_out.at[i], res_in.at[mine], r_send.at[i], r_recv.at[mine], at(side, t, pb)
        )
        copy.start()
        sends.append((None, copy))

    add(arrived[0], oy)
    add_rest(oy)
    give(0, oy, b)
    give(1, oy, ob)
    add(arrived[0], y)
    add_rest(y)
    give(2, y, ob)
    res_in[mine] = rows_of(y, b)
    for slot in (partner_slot, far_slot, far_partner):
        remote(
            res_in.at[slot], res_in.at[slot], r_send.at[0], r_recv.at[slot], at(y, t, ob)
        ).wait_recv()
    for c in range(4):
        wide = min(block, depth - c * block)
        out_ref[:, c * block : c * block + wide] = res_in[c, :, :wide]
    for condition, copy in sends:
        if condition is None:
            copy.wait_send()
        else:
            pl.when(condition)(copy.wait_send)


def fast_body(n, query_tokens, key_tokens, value_tokens, norm_gain, out_weight):
    frames, rows, width, depth = query_tokens.shape
    tokens = frames * rows * width
    shard_rows = out_weight.size // depth
    padded = round_up(shard_rows, 16)
    block = round_up(-(-depth // 4), LANES)
    half = round_up(-(-depth // 2), LANES)
    hops = n.bit_length() - 1
    main = shard_rows // LANES * LANES
    rest = padded - main
    flat = [x.reshape(tokens, depth) for x in (query_tokens, key_tokens, value_tokens)]
    f32, bf16 = jnp.float32, jnp.bfloat16
    packed = half + LANES
    dma = pltpu.SemaphoreType.DMA
    out = pl.pallas_call(
        functools.partial(kernel, n, shard_rows),
        out_shape=jax.ShapeDtypeStruct((tokens, depth), bf16),
        in_specs=[pl.BlockSpec(memory_space=pltpu.VMEM)] * 5,
        out_specs=pl.BlockSpec(memory_space=pltpu.VMEM),
        scratch_shapes=[
            pltpu.VMEM((out_weight.size // LANES, LANES), f32),
            pltpu.VMEM((4 * block // LANES, padded, LANES), f32),
            pltpu.VMEM((padded, 4 * block), bf16),
            pltpu.VMEM((2, HD, packed), f32),
            pltpu.VMEM((HD, packed), f32),
            pltpu.VMEM((HD, packed), bf16),
            pltpu.VMEM((HD, packed), bf16),
            pltpu.VMEM((hops, HD, packed), bf16),
            pltpu.VMEM((hops, HD, packed), bf16),
            pltpu.VMEM((2, HD, packed), bf16),
            pltpu.VMEM((tokens, depth), f32),
            pltpu.VMEM((2 * n, main, block), bf16),
            pltpu.VMEM((2 * n, rest, block), bf16),
            pltpu.VMEM((4, tokens, 2 * n * padded), bf16),
            pltpu.VMEM((2, 2 * tokens, block), f32),
            pltpu.VMEM((3, tokens, block), bf16),
            pltpu.VMEM((4, tokens, block), bf16),
            dma((2,)),
            dma((2 * n + 8,)),
            dma((2 * n,)),
            dma((2 * n + 8,)),
            dma((2 * n,)),
            dma((hops + 2,)),
            dma((hops + 2,)),
            dma((3,)),
            dma((4,)),
            dma((3,)),
            dma((4,)),
        ],
        compiler_params=pltpu.CompilerParams(
            collective_id=0, has_side_effects=True, vmem_limit_bytes=48 * 1024 * 1024
        ),
    )(*flat, norm_gain, out_weight)
    return out.reshape(query_tokens.shape)


def solution(mesh):
    n, bands, parts = mesh.shape["tm"], mesh.shape["band"], mesh.shape["parts"]

    def body(query_tokens, key_tokens, value_tokens, norm_gain, out_weight):
        depth = query_tokens.shape[3]
        ring = n >= 4 and n & (n - 1) == 0 and bands == 2 and parts == 2
        whole_pairs = out_weight.size % (2 * depth) == 0 and depth % LANES == LANES // 2
        few = round_up(-(-depth // 2), LANES) // LANES <= HD // 2
        ring = ring and LANES < out_weight.size // depth
        if ring and query_tokens.shape[0] == 1 and whole_pairs and few:
            return fast_body(n, query_tokens, key_tokens, value_tokens, norm_gain, out_weight)
        return plain_body(query_tokens, key_tokens, value_tokens, norm_gain, out_weight)

    spread = P(("parts", "tm"), "band", None, None)
    return jax.shard_map(
        body,
        mesh=mesh,
        in_specs=(spread, spread, spread, P(), P("band", "tm", None)),
        out_specs=spread,
        check_vma=False,
    )
```

```python
import functools

import jax
import jax.numpy as jnp
from jax import lax
from jax.experimental import pallas as pl
from jax.experimental.pallas import tpu as pltpu
from jax.sharding import PartitionSpec as P

HEADS = 70
HD = 32
LANES = 128

norm_epsilon = 1e-06
read_epsilon = 1e-06
MESH = pl.DeviceIdType.MESH


def round_up(x, m):
    return -(-x // m) * m


def core_widths(depth):
    tiles = -(-depth // LANES)
    chip = -(-tiles // 2)
    first = -(-chip // 2)
    return first * LANES, (chip - first) * LANES


def entering(x, axis):
    peers, place = (lax.axis_size(axis), lax.axis_index(axis))
    everything = jax.tree.map(lambda part: lax.all_gather(part, axis), x)

    def hop(k, before):
        return jax.tree.map(
            lambda a, part: jnp.where(k < place, a + part[k], a), before, everything
        )

    return lax.fori_loop(0, peers, hop, jax.tree.map(jnp.zeros_like, x))


def plain_body(query_tokens, key_tokens, value_tokens, norm_gain, out_weight):
    frames, rows, width, depth = query_tokens.shape
    key_relu = jax.nn.relu(key_tokens).reshape(frames, rows * width, HEADS, HD)
    value_heads = value_tokens.reshape(frames, rows * width, HEADS, HD)
    part_state = jnp.einsum(
        "fthd,fthe->fhde", key_relu, value_heads, preferred_element_type=jnp.float32
    ).reshape(frames, HEADS, HD * HD)
    part_norm = jnp.sum(key_relu, axis=1, dtype=jnp.float32)
    state_sum, norm_sum = lax.psum((part_state, part_norm), "band")
    local_state = jnp.cumsum(state_sum, axis=0)
    local_norm = jnp.cumsum(norm_sum, axis=0)
    before = entering((local_state[-1], local_norm[-1]), "tm")
    prefix_state = local_state + before[0]
    prefix_norm = local_norm + before[1]
    query_relu = jax.nn.relu(query_tokens.astype(jnp.float32)).reshape(
        frames, rows * width, HEADS, HD
    )
    numer = jnp.einsum(
        "fthd,fhde->fthe",
        query_relu,
        prefix_state.reshape(frames, HEADS, HD, HD),
        precision=lax.Precision.HIGHEST,
    )
    denom = (
        jnp.einsum("fthd,fhd->fth", query_relu, prefix_norm, precision=lax.Precision.HIGHEST)
        + read_epsilon
    )
    reads = (numer / denom[:, :, :, None]).reshape(frames * rows * width, depth)
    square = jnp.mean(reads * reads, axis=-1, keepdims=True)
    normed = (reads * lax.rsqrt(square + norm_epsilon) * norm_gain).astype(jnp.bfloat16)
    gathered = lax.all_gather(out_weight, "tm", axis=1, tiled=True)
    rows_half = gathered.reshape(-1, depth)
    result = jnp.dot(
        normed,
        lax.all_gather(rows_half, "band", axis=0, tiled=True),
        preferred_element_type=jnp.float32,
    )
    return result.astype(jnp.bfloat16).reshape(frames, rows, width, depth)


def kernel(
    n, shard_rows,
    q_hbm, k_hbm, v_hbm, g_hbm, flat_hbm, out_ref,
    q_ref, k_ref, v_ref, g_ref, flat_ref, in_sem, chunks_ref, w_wide, w_ref, state, own, band_out, band_in, hop_out, hop_in, final, reads,
    wbuf, wrest, abuf, acc, res_out, res_in,
    w_local_sem, w_send, w_recv, e_send, e_recv, s_send, s_recv, a_send, a_recv, r_send, r_recv,
):
    f32, bf16 = jnp.float32, jnp.bfloat16
    tokens, depth = q_ref.shape
    half = state.shape[2] - LANES
    block = wbuf.shape[2]
    widths = core_widths(depth)
    hops = n.bit_length() - 1
    groups = -(-depth // LANES)
    per_half = half // LANES

    loads = [
        pltpu.make_async_copy(src, dst, in_sem.at[i])
        for i, (src, dst) in enumerate(
            [(flat_hbm, flat_ref), (k_hbm, k_ref), (v_hbm, v_ref), (q_hbm, q_ref), (g_hbm, g_ref)]
        )
    ]
    for load in loads:
        load.start()

    y, t, b = lax.axis_index("parts"), lax.axis_index("tm"), lax.axis_index("band")
    oy, ob = 1 - y, 1 - b
    mine = y * 2 + b

    def at(py, pt, pb):
        return {"parts": py, "tm": pt, "band": pb}

    odd = t % 2
    pos = (1 - odd) * (t // 2) + odd * (n - 1 - t // 2)

    def chip(p):
        p = lax.rem(p + 2 * n, n)
        back = p // (n // 2)
        return (1 - back) * (2 * p) + back * (2 * (n - 1 - p) + 1)

    right, left = chip(pos + 1), chip(pos - 1)

    barrier = pltpu.get_barrier_semaphore()
    peers = [at(y, t, ob), at(oy, t, b), at(oy, t, ob)]
    for side in (right, left):
        peers += [at(y, side, b), at(y, side, ob)]
    for s in range(hops):
        d = 1 << s
        peers += [at(y, lax.rem(t + d, n), b), at(y, lax.rem(t + n - d, n), b)]
    for peer in peers:
        pl.semaphore_signal(barrier, inc=1, device_id=peer, device_id_type=MESH)

    loads[0].wait()
    size = flat_ref.shape[2]
    for lo in range(0, size, 8 * LANES):
        wide = min(8 * LANES, size - lo)
        chunks_ref[lo // LANES : (lo + wide) // LANES, :] = (
            flat_ref[0, :, lo : lo + wide].astype(f32).reshape(wide // LANES, LANES)
        )
    pairs, per_pair, tiles = shard_rows // 2, 2 * depth // LANES, -(-depth // LANES)
    w_wide[...] = jnp.zeros_like(w_wide)
    lower = lax.broadcasted_iota(jnp.int32, (pairs, LANES), 1) < LANES // 2

    def chunk(j):
        return chunks_ref[pl.ds(j, pairs, stride=per_pair), :]

    middle = chunk(tiles - 1)
    for j in range(tiles - 1):
        w_wide[j, pl.ds(0, pairs, stride=2), :] = chunk(j)
    w_wide[tiles - 1, pl.ds(0, pairs, stride=2), :] = jnp.where(lower, middle, 0.0)
    turned = pltpu.roll(middle, LANES // 2, 1)
    for j in range(tiles):
        if j + 1 < tiles:
            following = pltpu.roll(chunk(tiles + j), LANES // 2, 1)
        else:
            following = jnp.zeros_like(turned)
        w_wide[j, pl.ds(1, pairs, stride=2), :] = jnp.where(lower, turned, following)
        turned = following
    for j in range(w_wide.shape[0]):
        w_ref[:, j * LANES : (j + 1) * LANES] = w_wide[j].astype(bf16)
    pl.semaphore_wait(barrier, len(peers))

    def remote(src, dst, send, recv, peer):
        return pltpu.make_async_remote_copy(
            src_ref=src, dst_ref=dst, send_sem=send, recv_sem=recv,
            device_id=peer, device_id_type=MESH,
        )

    main = wbuf.shape[1]
    sends = []
    counter = [0]

    def columns(core, lo, size):
        start = pl.multiple_of(y * sum(widths) + core * widths[0], LANES)
        return w_ref.at[pl.ds(lo, size), pl.ds(start, widths[core])]

    def own_rows(core):
        return columns(core, 0, main), columns(core, main, wrest.shape[1])

    def held(slot):
        def at_width(core):
            return [buf.at[slot, :, pl.ds(0, widths[core])] for buf in (wbuf, wrest)]

        return at_width

    weight_sems = list(zip((w_send, e_send), (w_recv, e_recv)))

    def w_put(sources, slot, side, pb):
        i = counter[0]
        counter[0] += 1
        for core in range(2):
            for src, dst, (sent, got) in zip(sources(core), held(slot)(core), weight_sems):
                copy = remote(src, dst, sent.at[i], got.at[slot], at(y, side, pb))
                pl.when(pb == core)(copy.start)
                sends.append((pb == core, copy))

    def w_wait(slot):
        for core in range(2):
            for dst, (sent, got) in zip(held(slot)(core), weight_sems):
                copy = remote(dst, dst, sent.at[0], got.at[slot], at(y, t, ob))
                pl.when(b == core)(copy.wait_recv)

    me_slot = 2 * t + b
    for side in (right, left):
        w_put(own_rows, me_slot, side, b)
        w_put(own_rows, me_slot, side, ob)
    w_put(own_rows, me_slot, t, ob)
    locals_ = []
    for core in range(2):
        for i, (src, dst) in enumerate(zip(own_rows(core), held(me_slot)(core))):
            copy = pltpu.make_async_copy(src, dst, w_local_sem.at[i])
            pl.when(b == core)(copy.start)
            locals_.append((b == core, copy))
    arrived = []

    def forward(s, bands=(0, 1)):
        last = n // 2
        from_left, from_right = chip(pos - s), chip(pos + s)
        jobs = []
        if s < last:
            for beta in bands:
                jobs += [(2 * from_left + beta, right, s < last - 1 or beta == 0),
                         (2 * from_right + beta, left, s < last - 1 or beta == 1)]
            if bands[-1]:
                arrived.extend([from_left, from_right])
        else:
            jobs = [(2 * from_left, right, False), (2 * from_right + 1, left, False)]
            arrived.append(from_left)
        for slot, side, on in jobs:
            w_wait(slot)
            if on:
                w_put(held(slot), slot, side, b)

    rows = HD // 2

    def pack(x):
        sums = x[:rows, half:]
        hi = sums.astype(bf16).astype(f32)
        both = jnp.concatenate([hi, sums - hi], axis=0)
        return jnp.concatenate([x[:, :half], both], axis=1).astype(bf16)

    def unpack(x):
        x = x.astype(f32)
        sums = x[:rows, half:] + x[rows:, half:]
        sums = jnp.concatenate([sums, jnp.zeros_like(sums)], axis=0)
        return jnp.concatenate([x[:, :half], sums], axis=1)

    loads[1].wait()
    loads[2].wait()
    state[...] = jnp.zeros_like(state)
    ones = jnp.ones((8, tokens), bf16)
    for g in range(groups):
        lo, wide = g * LANES, min(LANES, depth - g * LANES)
        kg = jnp.maximum(k_ref[:, lo : lo + wide], 0)
        vg = v_ref[:, lo : lo + wide]
        full = lax.dot_general(kg, vg, (((0,), (0,)), ((), ())), preferred_element_type=f32)
        head = lax.broadcasted_iota(jnp.int32, (HD, wide), 1) // HD
        small = full[:HD]
        for h in range(1, wide // HD):
            small = jnp.where(head == h, full[h * HD : (h + 1) * HD], small)
        sums = jnp.dot(ones, kg, preferred_element_type=f32)
        where = pl.ds((g % per_half) * LANES, wide)
        state[g // per_half, :, where] = small
        row = g % per_half
        state[g // per_half, row : row + 1, half : half + wide] = sums[:1]

    band_out[...] = pack(state[ob])
    swap = remote(band_out, band_in, s_send.at[0], s_recv.at[0], at(y, t, ob))
    swap.start()
    sends.append((None, swap))
    swap.wait_recv()
    own[...] = state[b] + unpack(band_in[...])

    for s in range(hops):
        d = 1 << s
        hop = remote(
            hop_out.at[s], hop_in.at[s], s_send.at[1 + s], s_recv.at[1 + s],
            at(y, lax.rem(t + d, n), b),
        )
        hop_out[s] = pack(own[...])

        @pl.when(t + d < n)
        def _():
            hop.start()

        sends.append((t + d < n, hop))
        if s >= hops - 2:
            forward(1, (s - hops + 2,))

        @pl.when(t >= d)
        def _():
            hop.wait_recv()
            own[...] += unpack(hop_in[s])

    final[b] = pack(own[...])
    swap = remote(final.at[b], final.at[b], s_send.at[1 + hops], s_recv.at[1 + hops], at(y, t, ob))
    swap.start()
    sends.append((None, swap))
    swap.wait_recv()

    loads[3].wait()
    loads[4].wait()
    total = jnp.zeros((tokens, 1), f32)
    for g in range(groups):
        lo, wide = g * LANES, min(LANES, depth - g * LANES)
        qg = jnp.maximum(q_ref[:, lo : lo + wide], 0)
        packed = final[g // per_half, :, pl.ds((g % per_half) * LANES, wide)]
        same = (
            lax.broadcasted_iota(jnp.int32, (wide, wide), 0) // HD
            == lax.broadcasted_iota(jnp.int32, (wide, wide), 1) // HD
        )
        small = packed.astype(f32)
        tall = jnp.concatenate([small] * (wide // HD), axis=0)
        numer = jnp.dot(qg, jnp.where(same, tall, 0.0).astype(bf16), preferred_element_type=f32)
        sums = final[g // per_half, :, half : half + wide].astype(f32)
        row = g % per_half
        weigh = sums[row : row + 1] + sums[rows + row : rows + row + 1]
        terms = qg.astype(f32) * weigh
        hi = terms.astype(bf16)
        rest = (terms - hi.astype(f32)).astype(bf16)
        block_ones = jnp.where(same, 1.0, 0.0).astype(bf16)
        denom = (
            jnp.dot(hi, block_ones, preferred_element_type=f32)
            + jnp.dot(rest, block_ones, preferred_element_type=f32)
        )
        r = numer / (denom + read_epsilon)
        reads[:, lo : lo + wide] = r
        total = total + jnp.sum(r * r, axis=-1, keepdims=True)
    scale = lax.rsqrt(total * (1.0 / depth) + norm_epsilon)
    normed = reads[...] * scale * g_ref[...][None, :]
    shards, few = 2 * n, shard_rows - main
    gap = jnp.zeros((tokens, wrest.shape[1] - few), f32)
    extra = []
    for j in range(shards):
        slot, lo = 2 * (j % n) + j // n, j * shard_rows
        abuf[mine, :, slot * main : (slot + 1) * main] = normed[:, lo : lo + main].astype(bf16)
    for slot in range(shards):
        lo = (slot % 2 * n + slot // 2) * shard_rows + main
        extra += [normed[:, lo : lo + few], gap]
    abuf[mine, :, shards * main :] = jnp.concatenate(extra, axis=1).astype(bf16)

    partner_slot, far_slot, far_partner = y * 2 + ob, oy * 2 + b, oy * 2 + ob

    def a_put(slot, i, peer):
        copy = remote(abuf.at[slot], abuf.at[slot], a_send.at[i], a_recv.at[slot], peer)
        copy.start()
        sends.append((None, copy))

    def a_wait(slot):
        remote(abuf.at[slot], abuf.at[slot], a_send.at[0], a_recv.at[slot], at(y, t, ob)).wait_recv()

    a_put(mine, 0, at(oy, t, b))
    a_put(mine, 1, at(y, t, ob))

    if n > 4:
        forward(2)
    acc[...] = jnp.zeros_like(acc)
    a_wait(partner_slot)
    for s in range(3, n // 2):
        forward(s)
    for condition, copy in locals_:
        pl.when(condition)(copy.wait)
    w_wait(2 * t + ob)
    arrived.append(t)

    def add(p, side):
        lanes = pl.ds(pl.multiple_of(p * 2 * main, LANES), 2 * main)
        both = abuf[pl.ds(2 * side, 2), :, lanes].reshape(2 * tokens, 2 * main)
        rows = wbuf[pl.ds(2 * p, 2)].reshape(2 * main, block)
        acc[side] += jnp.dot(both, rows, preferred_element_type=f32)

    def add_rest(side):
        both = abuf[pl.ds(2 * side, 2), :, shards * main :].reshape(2 * tokens, -1)
        rows = wrest[...].reshape(-1, block)
        acc[side] += jnp.dot(both, rows, preferred_element_type=f32)

    for p in arrived:
        add(p, y)
    a_wait(far_slot)
    a_put(far_slot, 2, at(y, t, ob))
    a_wait(far_partner)
    for p in arrived:
        add(p, oy)
    arrived.clear()
    forward(n // 2)

    def rows_of(side, pb):
        return acc[side, pl.ds(pl.multiple_of(pb * tokens, 8), tokens), :].astype(bf16)

    def give(i, side, pb):
        res_out[i] = rows_of(side, pb)
        for core in range(2):
            lanes = pl.ds(0, widths[core])
            copy = remote(
                res_out.at[i, :, lanes], res_in.at[mine, :, lanes],
                r_send.at[i], r_recv.at[mine], at(side, t, pb),
            )
            pl.when(b == core)(copy.start)
            sends.append((b == core, copy))

    def take(slot, core):
        view = res_in.at[slot, :, pl.ds(0, widths[core])]
        remote(view, view, r_send.at[0], r_recv.at[slot], at(y, t, ob)).wait_recv()

    add(arrived[0], oy)
    add_rest(oy)
    give(0, oy, b)
    give(1, oy, ob)
    add(arrived[0], y)
    add_rest(y)
    give(2, y, ob)
    res_in[mine] = rows_of(y, b)
    for slot, pb in ((partner_slot, ob), (far_slot, b), (far_partner, ob)):
        for core in range(2):
            pl.when(pb == core)(functools.partial(take, slot, core))
    for c in range(4):
        start = c // 2 * sum(widths) + c % 2 * widths[0]
        wide = min(widths[c % 2], depth - start)
        out_ref[:, start : start + wide] = res_in[c, :, :wide]
    for condition, copy in sends:
        if condition is None:
            copy.wait_send()
        else:
            pl.when(condition)(copy.wait_send)


def fast_body(n, query_tokens, key_tokens, value_tokens, norm_gain, out_weight):
    frames, rows, width, depth = query_tokens.shape
    tokens = frames * rows * width
    shard_rows = out_weight.size // depth
    padded = round_up(shard_rows, 16)
    block = core_widths(depth)[0]
    half = round_up(-(-depth // 2), LANES)
    hops = n.bit_length() - 1
    main = shard_rows // LANES * LANES
    rest = padded - main
    wide = 2 * sum(core_widths(depth))
    flat = [x.reshape(tokens, depth) for x in (query_tokens, key_tokens, value_tokens)]
    f32, bf16 = jnp.float32, jnp.bfloat16
    packed = half + LANES
    dma = pltpu.SemaphoreType.DMA
    out = pl.pallas_call(
        functools.partial(kernel, n, shard_rows),
        out_shape=jax.ShapeDtypeStruct((tokens, depth), bf16),
        in_specs=[pl.BlockSpec(memory_space=pltpu.HBM)] * 5,
        out_specs=pl.BlockSpec(memory_space=pltpu.VMEM),
        scratch_shapes=[
            *[pltpu.VMEM((tokens, depth), bf16)] * 3,
            pltpu.VMEM((depth,), f32),
            pltpu.VMEM(out_weight.shape, bf16),
            dma((5,)),
            pltpu.VMEM((out_weight.size // LANES, LANES), f32),
            pltpu.VMEM((wide // LANES, padded, LANES), f32),
            pltpu.VMEM((padded, wide), bf16),
            pltpu.VMEM((2, HD, packed), f32),
            pltpu.VMEM((HD, packed), f32),
            pltpu.VMEM((HD, packed), bf16),
            pltpu.VMEM((HD, packed), bf16),
            pltpu.VMEM((hops, HD, packed), bf16),
            pltpu.VMEM((hops, HD, packed), bf16),
            pltpu.VMEM((2, HD, packed), bf16),
            pltpu.VMEM((tokens, depth), f32),
            pltpu.VMEM((2 * n, main, block), bf16),
            pltpu.VMEM((2 * n, rest, block), bf16),
            pltpu.VMEM((4, tokens, 2 * n * padded), bf16),
            pltpu.VMEM((2, 2 * tokens, block), f32),
            pltpu.VMEM((3, tokens, block), bf16),
            pltpu.VMEM((4, tokens, block), bf16),
            dma((2,)),
            dma((2 * n + 8,)),
            dma((2 * n,)),
            dma((2 * n + 8,)),
            dma((2 * n,)),
            dma((hops + 2,)),
            dma((hops + 2,)),
            dma((3,)),
            dma((4,)),
            dma((3,)),
            dma((4,)),
        ],
        compiler_params=pltpu.CompilerParams(
            collective_id=0, has_side_effects=True, vmem_limit_bytes=63 * 1024 * 1024
        ),
    )(*flat, norm_gain, out_weight)
    return out.reshape(query_tokens.shape)


def solution(mesh):
    n, bands, parts = mesh.shape["tm"], mesh.shape["band"], mesh.shape["parts"]

    def body(query_tokens, key_tokens, value_tokens, norm_gain, out_weight):
        depth = query_tokens.shape[3]
        ring = n >= 4 and n & (n - 1) == 0 and bands == 2 and parts == 2
        whole_pairs = out_weight.size % (2 * depth) == 0 and depth % LANES == LANES // 2
        few = round_up(-(-depth // 2), LANES) // LANES <= HD // 2
        ring = ring and LANES < out_weight.size // depth
        if ring and query_tokens.shape[0] == 1 and whole_pairs and few:
            return fast_body(n, query_tokens, key_tokens, value_tokens, norm_gain, out_weight)
        return plain_body(query_tokens, key_tokens, value_tokens, norm_gain, out_weight)

    spread = P(("parts", "tm"), "band", None, None)
    return jax.shard_map(
        body,
        mesh=mesh,
        in_specs=(spread, spread, spread, P(), P("band", "tm", None)),
        out_specs=spread,
        check_vma=False,
    )
```

```python
import functools

import jax
import jax.numpy as jnp
from jax import lax
from jax.experimental import pallas as pl
from jax.experimental.pallas import tpu as pltpu
from jax.sharding import PartitionSpec as P

HEADS = 70
HD = 32
LANES = 128

norm_epsilon = 1e-06
read_epsilon = 1e-06
MESH = pl.DeviceIdType.MESH


def round_up(x, m):
    return -(-x // m) * m


def core_widths(depth):
    tiles = -(-depth // LANES)
    chip = -(-tiles // 2)
    first = -(-chip // 2)
    return first * LANES, (chip - first) * LANES


def entering(x, axis):
    peers, place = (lax.axis_size(axis), lax.axis_index(axis))
    everything = jax.tree.map(lambda part: lax.all_gather(part, axis), x)

    def hop(k, before):
        return jax.tree.map(
            lambda a, part: jnp.where(k < place, a + part[k], a), before, everything
        )

    return lax.fori_loop(0, peers, hop, jax.tree.map(jnp.zeros_like, x))


def plain_body(query_tokens, key_tokens, value_tokens, norm_gain, out_weight):
    frames, rows, width, depth = query_tokens.shape
    key_relu = jax.nn.relu(key_tokens).reshape(frames, rows * width, HEADS, HD)
    value_heads = value_tokens.reshape(frames, rows * width, HEADS, HD)
    part_state = jnp.einsum(
        "fthd,fthe->fhde", key_relu, value_heads, preferred_element_type=jnp.float32
    ).reshape(frames, HEADS, HD * HD)
    part_norm = jnp.sum(key_relu, axis=1, dtype=jnp.float32)
    state_sum, norm_sum = lax.psum((part_state, part_norm), "band")
    local_state = jnp.cumsum(state_sum, axis=0)
    local_norm = jnp.cumsum(norm_sum, axis=0)
    before = entering((local_state[-1], local_norm[-1]), "tm")
    prefix_state = local_state + before[0]
    prefix_norm = local_norm + before[1]
    query_relu = jax.nn.relu(query_tokens.astype(jnp.float32)).reshape(
        frames, rows * width, HEADS, HD
    )
    numer = jnp.einsum(
        "fthd,fhde->fthe",
        query_relu,
        prefix_state.reshape(frames, HEADS, HD, HD),
        precision=lax.Precision.HIGHEST,
    )
    denom = (
        jnp.einsum("fthd,fhd->fth", query_relu, prefix_norm, precision=lax.Precision.HIGHEST)
        + read_epsilon
    )
    reads = (numer / denom[:, :, :, None]).reshape(frames * rows * width, depth)
    square = jnp.mean(reads * reads, axis=-1, keepdims=True)
    normed = (reads * lax.rsqrt(square + norm_epsilon) * norm_gain).astype(jnp.bfloat16)
    gathered = lax.all_gather(out_weight, "tm", axis=1, tiled=True)
    rows_half = gathered.reshape(-1, depth)
    result = jnp.dot(
        normed,
        lax.all_gather(rows_half, "band", axis=0, tiled=True),
        preferred_element_type=jnp.float32,
    )
    return result.astype(jnp.bfloat16).reshape(frames, rows, width, depth)


def kernel(
    n, shard_rows,
    q_hbm, k_hbm, v_hbm, g_hbm, flat_hbm, out_ref,
    q_ref, k_ref, v_ref, g_ref, flat_ref, in_sem, chunks_ref, w_wide, w_ref, state, own, band_out, band_in, hop_out, hop_in, final, reads,
    wbuf, wrest, abuf, acc, res_out, res_in,
    w_local_sem, w_send, w_recv, e_send, e_recv, s_send, s_recv, a_send, a_recv, r_send, r_recv,
):
    f32, bf16 = jnp.float32, jnp.bfloat16
    tokens, depth = q_ref.shape
    half = state.shape[2] - LANES
    block = wbuf.shape[2]
    widths = core_widths(depth)
    hops = n.bit_length() - 1
    groups = -(-depth // LANES)
    per_half = half // LANES

    loads = [
        pltpu.make_async_copy(src, dst, in_sem.at[i])
        for i, (src, dst) in enumerate(
            [(k_hbm, k_ref), (v_hbm, v_ref), (flat_hbm, flat_ref), (q_hbm, q_ref), (g_hbm, g_ref)]
        )
    ]
    for load in loads:
        load.start()

    y, t, b = lax.axis_index("parts"), lax.axis_index("tm"), lax.axis_index("band")
    oy, ob = 1 - y, 1 - b
    mine = y * 2 + b

    def at(py, pt, pb):
        return {"parts": py, "tm": pt, "band": pb}

    odd = t % 2
    pos = (1 - odd) * (t // 2) + odd * (n - 1 - t // 2)

    def chip(p):
        p = lax.rem(p + 2 * n, n)
        back = p // (n // 2)
        return (1 - back) * (2 * p) + back * (2 * (n - 1 - p) + 1)

    right, left = chip(pos + 1), chip(pos - 1)

    barrier = pltpu.get_barrier_semaphore()
    peers = [at(y, t, ob), at(oy, t, b), at(oy, t, ob)]
    for side in (right, left):
        peers += [at(y, side, b), at(y, side, ob)]
    for s in range(hops):
        d = 1 << s
        peers += [at(y, lax.rem(t + d, n), b), at(y, lax.rem(t + n - d, n), b)]
    for peer in peers:
        pl.semaphore_signal(barrier, inc=1, device_id=peer, device_id_type=MESH)

    pl.semaphore_wait(barrier, len(peers))

    def remote(src, dst, send, recv, peer):
        return pltpu.make_async_remote_copy(
            src_ref=src, dst_ref=dst, send_sem=send, recv_sem=recv,
            device_id=peer, device_id_type=MESH,
        )

    main = wbuf.shape[1]
    sends = []
    counter = [0]

    def columns(core, lo, size):
        start = pl.multiple_of(y * sum(widths) + core * widths[0], LANES)
        return w_ref.at[pl.ds(lo, size), pl.ds(start, widths[core])]

    def own_rows(core):
        return columns(core, 0, main), columns(core, main, wrest.shape[1])

    def held(slot):
        def at_width(core):
            return [buf.at[slot, :, pl.ds(0, widths[core])] for buf in (wbuf, wrest)]

        return at_width

    weight_sems = list(zip((w_send, e_send), (w_recv, e_recv)))

    def w_put(sources, slot, side, pb):
        i = counter[0]
        counter[0] += 1
        for core in range(2):
            for src, dst, (sent, got) in zip(sources(core), held(slot)(core), weight_sems):
                copy = remote(src, dst, sent.at[i], got.at[slot], at(y, side, pb))
                pl.when(pb == core)(copy.start)
                sends.append((pb == core, copy))

    def w_wait(slot):
        for core in range(2):
            for dst, (sent, got) in zip(held(slot)(core), weight_sems):
                copy = remote(dst, dst, sent.at[0], got.at[slot], at(y, t, ob))
                pl.when(b == core)(copy.wait_recv)

    me_slot = 2 * t + b
    locals_ = [
        (b == core, pltpu.make_async_copy(src, dst, w_local_sem.at[i]))
        for core in range(2)
        for i, (src, dst) in enumerate(zip(own_rows(core), held(me_slot)(core)))
    ]

    def first_step(pb):
        for side in (right, left):
            w_put(own_rows, me_slot, side, pb)

    arrived = []

    def forward(s, bands=(0, 1)):
        last = n // 2
        from_left, from_right = chip(pos - s), chip(pos + s)
        jobs = []
        if s < last:
            for beta in bands:
                jobs += [(2 * from_left + beta, right, s < last - 1 or beta == 0),
                         (2 * from_right + beta, left, s < last - 1 or beta == 1)]
            if len(bands) == 2:
                arrived.extend([from_left, from_right])
        else:
            jobs = [(2 * from_left, right, False), (2 * from_right + 1, left, False)]
            arrived.append(from_left)
        for slot, side, on in jobs:
            w_wait(slot)
            if on:
                w_put(held(slot), slot, side, b)

    rows = HD // 2

    def pack(x):
        sums = x[:rows, half:]
        hi = sums.astype(bf16).astype(f32)
        both = jnp.concatenate([hi, sums - hi], axis=0)
        return jnp.concatenate([x[:, :half], both], axis=1).astype(bf16)

    def unpack(x):
        x = x.astype(f32)
        sums = x[:rows, half:] + x[rows:, half:]
        sums = jnp.concatenate([sums, jnp.zeros_like(sums)], axis=0)
        return jnp.concatenate([x[:, :half], sums], axis=1)

    loads[0].wait()
    loads[1].wait()
    state[...] = jnp.zeros_like(state)
    ones = jnp.ones((8, tokens), bf16)
    for g in range(groups):
        lo, wide = g * LANES, min(LANES, depth - g * LANES)
        kg = jnp.maximum(k_ref[:, lo : lo + wide], 0)
        vg = v_ref[:, lo : lo + wide]
        full = lax.dot_general(kg, vg, (((0,), (0,)), ((), ())), preferred_element_type=f32)
        head = lax.broadcasted_iota(jnp.int32, (HD, wide), 1) // HD
        small = full[:HD]
        for h in range(1, wide // HD):
            small = jnp.where(head == h, full[h * HD : (h + 1) * HD], small)
        sums = jnp.dot(ones, kg, preferred_element_type=f32)
        where = pl.ds((g % per_half) * LANES, wide)
        state[g // per_half, :, where] = small
        row = g % per_half
        state[g // per_half, row : row + 1, half : half + wide] = sums[:1]

    band_out[...] = pack(state[ob])
    swap = remote(band_out, band_in, s_send.at[0], s_recv.at[0], at(y, t, ob))
    swap.start()
    sends.append((None, swap))

    loads[2].wait()
    size = flat_ref.shape[2]
    for lo in range(0, size, 8 * LANES):
        wide = min(8 * LANES, size - lo)
        chunks_ref[lo // LANES : (lo + wide) // LANES, :] = (
            flat_ref[0, :, lo : lo + wide].astype(f32).reshape(wide // LANES, LANES)
        )
    pairs, per_pair, tiles = shard_rows // 2, 2 * depth // LANES, -(-depth // LANES)
    w_wide[...] = jnp.zeros_like(w_wide)
    lower = lax.broadcasted_iota(jnp.int32, (pairs, LANES), 1) < LANES // 2

    def chunk(j):
        return chunks_ref[pl.ds(j, pairs, stride=per_pair), :]

    middle = chunk(tiles - 1)
    for j in range(tiles - 1):
        w_wide[j, pl.ds(0, pairs, stride=2), :] = chunk(j)
    w_wide[tiles - 1, pl.ds(0, pairs, stride=2), :] = jnp.where(lower, middle, 0.0)
    turned = pltpu.roll(middle, LANES // 2, 1)
    for j in range(tiles):
        if j + 1 < tiles:
            following = pltpu.roll(chunk(tiles + j), LANES // 2, 1)
        else:
            following = jnp.zeros_like(turned)
        w_wide[j, pl.ds(1, pairs, stride=2), :] = jnp.where(lower, turned, following)
        turned = following
    for j in range(w_wide.shape[0]):
        w_ref[:, j * LANES : (j + 1) * LANES] = w_wide[j].astype(bf16)
    for condition, copy in locals_:
        pl.when(condition)(copy.start)
    swap.wait_recv()
    own[...] = state[b] + unpack(band_in[...])

    for s in range(hops):
        d = 1 << s
        hop = remote(
            hop_out.at[s], hop_in.at[s], s_send.at[1 + s], s_recv.at[1 + s],
            at(y, lax.rem(t + d, n), b),
        )
        hop_out[s] = pack(own[...])

        @pl.when(t + d < n)
        def _():
            hop.start()

        sends.append((t + d < n, hop))
        if s == 0:
            first_step(b)
        elif s == 1:
            first_step(ob)
            w_put(own_rows, me_slot, t, ob)
        elif s == 2:
            forward(1, (b,))

        @pl.when(t >= d)
        def _():
            hop.wait_recv()
            own[...] += unpack(hop_in[s])

    final[b] = pack(own[...])
    swap = remote(final.at[b], final.at[b], s_send.at[1 + hops], s_recv.at[1 + hops], at(y, t, ob))
    swap.start()
    sends.append((None, swap))
    forward(1, (ob,))
    arrived += [chip(pos - 1), chip(pos + 1)]
    swap.wait_recv()

    loads[3].wait()
    loads[4].wait()
    partner_slot, far_slot, far_partner = y * 2 + ob, oy * 2 + b, oy * 2 + ob
    shards, few = 2 * n, shard_rows - main
    part = tokens // 2

    def piece(slot, h):
        return abuf.at[slot, pl.ds(h * part, part), :]

    def a_put(slot, h, i, peer):
        view = piece(slot, h)
        copy = remote(view, view, a_send.at[i, h], a_recv.at[slot, h], peer)
        copy.start()
        sends.append((None, copy))

    def a_wait(slot, h):
        view = piece(slot, h)
        remote(view, view, a_send.at[0, h], a_recv.at[slot, h], at(y, t, ob)).wait_recv()

    for h in range(2):
        top = h * part
        total = jnp.zeros((part, 1), f32)
        for g in range(groups):
            lo, wide = g * LANES, min(LANES, depth - g * LANES)
            row = g % per_half
            qg = jnp.maximum(q_ref[top : top + part, lo : lo + wide], 0)
            small = final[g // per_half, :, pl.ds(row * LANES, wide)].astype(f32)
            same = (
                lax.broadcasted_iota(jnp.int32, (wide, wide), 0) // HD
                == lax.broadcasted_iota(jnp.int32, (wide, wide), 1) // HD
            )
            tall = jnp.concatenate([small] * (wide // HD), axis=0)
            numer = jnp.dot(qg, jnp.where(same, tall, 0.0).astype(bf16), preferred_element_type=f32)
            sums = final[g // per_half, :, half : half + wide].astype(f32)
            weigh = sums[row : row + 1] + sums[rows + row : rows + row + 1]
            terms = qg.astype(f32) * weigh
            hi = terms.astype(bf16)
            rest = (terms - hi.astype(f32)).astype(bf16)
            block_ones = jnp.where(same, 1.0, 0.0).astype(bf16)
            both = jnp.concatenate([hi, rest], axis=0)
            denom = jnp.dot(both, block_ones, preferred_element_type=f32)
            r = numer / (denom[:part] + denom[part:] + read_epsilon)
            reads[top : top + part, lo : lo + wide] = r
            total = total + jnp.sum(r * r, axis=-1, keepdims=True)
        scale = lax.rsqrt(total * (1.0 / depth) + norm_epsilon)
        normed = reads[top : top + part, :] * scale * g_ref[...][None, :]
        gap = jnp.zeros((part, wrest.shape[1] - few), f32)
        extra = []
        for slot in range(shards):
            lo = (slot % 2 * n + slot // 2) * shard_rows
            abuf[mine, top : top + part, slot * main : (slot + 1) * main] = normed[
                :, lo : lo + main
            ].astype(bf16)
            extra += [normed[:, lo + main : lo + shard_rows], gap]
        abuf[mine, top : top + part, shards * main :] = jnp.concatenate(extra, axis=1).astype(bf16)
        a_put(mine, h, 0, at(oy, t, b))
        a_put(mine, h, 1, at(y, t, ob))

    if n > 4:
        forward(2)
    acc[...] = jnp.zeros_like(acc)
    for h in range(2):
        a_wait(partner_slot, h)
    for s in range(3, n // 2):
        forward(s)
    for condition, copy in locals_:
        pl.when(condition)(copy.wait)
    w_wait(2 * t + ob)
    arrived.append(t)

    def add(p, side):
        lanes = pl.ds(pl.multiple_of(p * 2 * main, LANES), 2 * main)
        both = abuf[pl.ds(2 * side, 2), :, lanes].reshape(2 * tokens, 2 * main)
        rows = wbuf[pl.ds(2 * p, 2)].reshape(2 * main, block)
        acc[side] += jnp.dot(both, rows, preferred_element_type=f32)

    def add_rest(side):
        both = abuf[pl.ds(2 * side, 2), :, shards * main :].reshape(2 * tokens, -1)
        rows = wrest[...].reshape(-1, block)
        acc[side] += jnp.dot(both, rows, preferred_element_type=f32)

    for p in arrived:
        add(p, y)
    for h in range(2):
        a_wait(far_slot, h)
        a_put(far_slot, h, 2, at(y, t, ob))
    for h in range(2):
        a_wait(far_partner, h)
    for p in arrived:
        add(p, oy)
    arrived.clear()
    forward(n // 2)

    def rows_of(side, pb):
        return acc[side, pl.ds(pl.multiple_of(pb * tokens, 8), tokens), :].astype(bf16)

    def give(i, side, pb):
        res_out[i] = rows_of(side, pb)
        for core in range(2):
            lanes = pl.ds(0, widths[core])
            copy = remote(
                res_out.at[i, :, lanes], res_in.at[mine, :, lanes],
                r_send.at[i], r_recv.at[mine], at(side, t, pb),
            )
            pl.when(b == core)(copy.start)
            sends.append((b == core, copy))

    def take(slot, core):
        view = res_in.at[slot, :, pl.ds(0, widths[core])]
        remote(view, view, r_send.at[0], r_recv.at[slot], at(y, t, ob)).wait_recv()

    add(arrived[0], oy)
    add_rest(oy)
    give(0, oy, b)
    give(1, oy, ob)
    add(arrived[0], y)
    add_rest(y)
    give(2, y, ob)
    res_in[mine] = rows_of(y, b)
    for slot, pb in ((partner_slot, ob), (far_slot, b), (far_partner, ob)):
        for core in range(2):
            pl.when(pb == core)(functools.partial(take, slot, core))
    for c in range(4):
        start = c // 2 * sum(widths) + c % 2 * widths[0]
        wide = min(widths[c % 2], depth - start)
        out_ref[:, start : start + wide] = res_in[c, :, :wide]
    for condition, copy in sends:
        if condition is None:
            copy.wait_send()
        else:
            pl.when(condition)(copy.wait_send)


def fast_body(n, query_tokens, key_tokens, value_tokens, norm_gain, out_weight):
    frames, rows, width, depth = query_tokens.shape
    tokens = frames * rows * width
    shard_rows = out_weight.size // depth
    padded = round_up(shard_rows, 16)
    block = core_widths(depth)[0]
    half = round_up(-(-depth // 2), LANES)
    hops = n.bit_length() - 1
    main = shard_rows // LANES * LANES
    rest = padded - main
    wide = 2 * sum(core_widths(depth))
    flat = [x.reshape(tokens, depth) for x in (query_tokens, key_tokens, value_tokens)]
    f32, bf16 = jnp.float32, jnp.bfloat16
    packed = half + LANES
    dma = pltpu.SemaphoreType.DMA
    out = pl.pallas_call(
        functools.partial(kernel, n, shard_rows),
        out_shape=jax.ShapeDtypeStruct((tokens, depth), bf16),
        in_specs=[pl.BlockSpec(memory_space=pltpu.HBM)] * 5,
        out_specs=pl.BlockSpec(memory_space=pltpu.VMEM),
        scratch_shapes=[
            *[pltpu.VMEM((tokens, depth), bf16)] * 3,
            pltpu.VMEM((depth,), f32),
            pltpu.VMEM(out_weight.shape, bf16),
            dma((5,)),
            pltpu.VMEM((out_weight.size // LANES, LANES), f32),
            pltpu.VMEM((wide // LANES, padded, LANES), f32),
            pltpu.VMEM((padded, wide), bf16),
            pltpu.VMEM((2, HD, packed), f32),
            pltpu.VMEM((HD, packed), f32),
            pltpu.VMEM((HD, packed), bf16),
            pltpu.VMEM((HD, packed), bf16),
            pltpu.VMEM((hops, HD, packed), bf16),
            pltpu.VMEM((hops, HD, packed), bf16),
            pltpu.VMEM((2, HD, packed), bf16),
            pltpu.VMEM((tokens, depth), f32),
            pltpu.VMEM((2 * n, main, block), bf16),
            pltpu.VMEM((2 * n, rest, block), bf16),
            pltpu.VMEM((4, tokens, 2 * n * padded), bf16),
            pltpu.VMEM((2, 2 * tokens, block), f32),
            pltpu.VMEM((3, tokens, block), bf16),
            pltpu.VMEM((4, tokens, block), bf16),
            dma((2,)),
            dma((2 * n + 8,)),
            dma((2 * n,)),
            dma((2 * n + 8,)),
            dma((2 * n,)),
            dma((hops + 2,)),
            dma((hops + 2,)),
            dma((3, 2)),
            dma((4, 2)),
            dma((3,)),
            dma((4,)),
        ],
        compiler_params=pltpu.CompilerParams(
            collective_id=0, has_side_effects=True, vmem_limit_bytes=63 * 1024 * 1024
        ),
    )(*flat, norm_gain, out_weight)
    return out.reshape(query_tokens.shape)


def solution(mesh):
    n, bands, parts = mesh.shape["tm"], mesh.shape["band"], mesh.shape["parts"]

    def body(query_tokens, key_tokens, value_tokens, norm_gain, out_weight):
        depth = query_tokens.shape[3]
        ring = n >= 8 and n & (n - 1) == 0 and bands == 2 and parts == 2
        whole_pairs = out_weight.size % (2 * depth) == 0 and depth % LANES == LANES // 2
        few = round_up(-(-depth // 2), LANES) // LANES <= HD // 2
        ring = ring and LANES < out_weight.size // depth
        if ring and query_tokens.shape[0] == 1 and whole_pairs and few:
            return fast_body(n, query_tokens, key_tokens, value_tokens, norm_gain, out_weight)
        return plain_body(query_tokens, key_tokens, value_tokens, norm_gain, out_weight)

    spread = P(("parts", "tm"), "band", None, None)
    return jax.shard_map(
        body,
        mesh=mesh,
        in_specs=(spread, spread, spread, P(), P("band", "tm", None)),
        out_specs=spread,
        check_vma=False,
    )
```

```python
import functools

import jax
import jax.numpy as jnp
from jax import lax
from jax.experimental import pallas as pl
from jax.experimental.pallas import tpu as pltpu
from jax.sharding import PartitionSpec as P

HEADS = 70
HD = 32
LANES = 128

norm_epsilon = 1e-06
read_epsilon = 1e-06
MESH = pl.DeviceIdType.MESH


def round_up(x, m):
    return -(-x // m) * m


def core_widths(depth):
    tiles = -(-depth // LANES)
    chip = -(-tiles // 2)
    first = -(-chip // 2)
    return first * LANES, (chip - first) * LANES


def entering(x, axis):
    peers, place = (lax.axis_size(axis), lax.axis_index(axis))
    everything = jax.tree.map(lambda part: lax.all_gather(part, axis), x)

    def hop(k, before):
        return jax.tree.map(
            lambda a, part: jnp.where(k < place, a + part[k], a), before, everything
        )

    return lax.fori_loop(0, peers, hop, jax.tree.map(jnp.zeros_like, x))


def plain_body(query_tokens, key_tokens, value_tokens, norm_gain, out_weight):
    frames, rows, width, depth = query_tokens.shape
    key_relu = jax.nn.relu(key_tokens).reshape(frames, rows * width, HEADS, HD)
    value_heads = value_tokens.reshape(frames, rows * width, HEADS, HD)
    part_state = jnp.einsum(
        "fthd,fthe->fhde", key_relu, value_heads, preferred_element_type=jnp.float32
    ).reshape(frames, HEADS, HD * HD)
    part_norm = jnp.sum(key_relu, axis=1, dtype=jnp.float32)
    state_sum, norm_sum = lax.psum((part_state, part_norm), "band")
    local_state = jnp.cumsum(state_sum, axis=0)
    local_norm = jnp.cumsum(norm_sum, axis=0)
    before = entering((local_state[-1], local_norm[-1]), "tm")
    prefix_state = local_state + before[0]
    prefix_norm = local_norm + before[1]
    query_relu = jax.nn.relu(query_tokens.astype(jnp.float32)).reshape(
        frames, rows * width, HEADS, HD
    )
    numer = jnp.einsum(
        "fthd,fhde->fthe",
        query_relu,
        prefix_state.reshape(frames, HEADS, HD, HD),
        precision=lax.Precision.HIGHEST,
    )
    denom = (
        jnp.einsum("fthd,fhd->fth", query_relu, prefix_norm, precision=lax.Precision.HIGHEST)
        + read_epsilon
    )
    reads = (numer / denom[:, :, :, None]).reshape(frames * rows * width, depth)
    square = jnp.mean(reads * reads, axis=-1, keepdims=True)
    normed = (reads * lax.rsqrt(square + norm_epsilon) * norm_gain).astype(jnp.bfloat16)
    gathered = lax.all_gather(out_weight, "tm", axis=1, tiled=True)
    rows_half = gathered.reshape(-1, depth)
    result = jnp.dot(
        normed,
        lax.all_gather(rows_half, "band", axis=0, tiled=True),
        preferred_element_type=jnp.float32,
    )
    return result.astype(jnp.bfloat16).reshape(frames, rows, width, depth)


def kernel(
    n, shard_rows,
    q_hbm, k_hbm, v_hbm, g_hbm, flat_hbm, out_ref,
    q_ref, k_ref, v_ref, g_ref, flat_ref, in_sem, chunks_ref, w_wide, w_ref, state, own, band_out, band_in, hop_out, hop_in, final, reads,
    wbuf, wrest, abuf, acc, res_out, res_in,
    w_local_sem, w_send, w_recv, e_send, e_recv, s_send, s_recv, a_send, a_recv, r_send, r_recv,
):
    f32, bf16 = jnp.float32, jnp.bfloat16
    tokens, depth = q_ref.shape
    half = state.shape[2] - LANES
    block = wbuf.shape[2]
    widths = core_widths(depth)
    hops = n.bit_length() - 1
    groups = -(-depth // LANES)
    per_half = half // LANES

    loads = [
        pltpu.make_async_copy(src, dst, in_sem.at[i])
        for i, (src, dst) in enumerate(
            [(k_hbm, k_ref), (v_hbm, v_ref), (flat_hbm, flat_ref), (q_hbm, q_ref), (g_hbm, g_ref)]
        )
    ]
    for load in loads:
        load.start()

    y, t, b = lax.axis_index("parts"), lax.axis_index("tm"), lax.axis_index("band")
    oy, ob = 1 - y, 1 - b
    mine = y * 2 + b

    def at(py, pt, pb):
        return {"parts": py, "tm": pt, "band": pb}

    odd = t % 2
    pos = (1 - odd) * (t // 2) + odd * (n - 1 - t // 2)

    def chip(p):
        p = lax.rem(p + 2 * n, n)
        back = p // (n // 2)
        return (1 - back) * (2 * p) + back * (2 * (n - 1 - p) + 1)

    right, left = chip(pos + 1), chip(pos - 1)

    barrier = pltpu.get_barrier_semaphore()
    peers = [at(y, t, ob), at(oy, t, b), at(oy, t, ob)]
    for side in (right, left):
        peers += [at(y, side, b), at(y, side, ob)]
    for s in range(hops):
        d = 1 << s
        peers += [at(y, lax.rem(t + d, n), b), at(y, lax.rem(t + n - d, n), b)]
    for peer in peers:
        pl.semaphore_signal(barrier, inc=1, device_id=peer, device_id_type=MESH)

    pl.semaphore_wait(barrier, len(peers))

    def remote(src, dst, send, recv, peer):
        return pltpu.make_async_remote_copy(
            src_ref=src, dst_ref=dst, send_sem=send, recv_sem=recv,
            device_id=peer, device_id_type=MESH,
        )

    main = wbuf.shape[1]
    sends = []
    counter = [0]

    def columns(core, lo, size):
        start = pl.multiple_of(y * sum(widths) + core * widths[0], LANES)
        return w_ref.at[pl.ds(lo, size), pl.ds(start, widths[core])]

    def own_rows(core):
        return columns(core, 0, main), columns(core, main, wrest.shape[1])

    def held(slot):
        def at_width(core):
            return [buf.at[slot, :, pl.ds(0, widths[core])] for buf in (wbuf, wrest)]

        return at_width

    weight_sems = list(zip((w_send, e_send), (w_recv, e_recv)))

    def w_put(sources, slot, side, pb):
        i = counter[0]
        counter[0] += 1
        for core in range(2):
            for src, dst, (sent, got) in zip(sources(core), held(slot)(core), weight_sems):
                copy = remote(src, dst, sent.at[i], got.at[slot], at(y, side, pb))
                pl.when(pb == core)(copy.start)
                sends.append((pb == core, copy))

    def w_wait(slot):
        for core in range(2):
            for dst, (sent, got) in zip(held(slot)(core), weight_sems):
                copy = remote(dst, dst, sent.at[0], got.at[slot], at(y, t, ob))
                pl.when(b == core)(copy.wait_recv)

    me_slot = 2 * t + b
    locals_ = [
        (b == core, pltpu.make_async_copy(src, dst, w_local_sem.at[i]))
        for core in range(2)
        for i, (src, dst) in enumerate(zip(own_rows(core), held(me_slot)(core)))
    ]

    def first_step(pb):
        for side in (right, left):
            w_put(own_rows, me_slot, side, pb)

    arrived = []

    def forward(s, bands=(0, 1)):
        last = n // 2
        from_left, from_right = chip(pos - s), chip(pos + s)
        jobs = []
        if s < last:
            for beta in bands:
                jobs += [(2 * from_left + beta, right, s < last - 1 or beta == 0),
                         (2 * from_right + beta, left, s < last - 1 or beta == 1)]
            if len(bands) == 2:
                arrived.extend([from_left, from_right])
        else:
            jobs = [(2 * from_left, right, False), (2 * from_right + 1, left, False)]
            arrived.append(from_left)
        for slot, side, on in jobs:
            w_wait(slot)
            if on:
                w_put(held(slot), slot, side, b)

    rows = HD // 2

    def pack(x):
        sums = x[:rows, half:]
        hi = sums.astype(bf16).astype(f32)
        both = jnp.concatenate([hi, sums - hi], axis=0)
        return jnp.concatenate([x[:, :half], both], axis=1).astype(bf16)

    def unpack(x):
        x = x.astype(f32)
        sums = x[:rows, half:] + x[rows:, half:]
        sums = jnp.concatenate([sums, jnp.zeros_like(sums)], axis=0)
        return jnp.concatenate([x[:, :half], sums], axis=1)

    loads[0].wait()
    loads[1].wait()
    state[...] = jnp.zeros_like(state)
    ones = jnp.ones((8, tokens), bf16)
    for g in range(groups):
        lo, wide = g * LANES, min(LANES, depth - g * LANES)
        kg = jnp.maximum(k_ref[:, lo : lo + wide], 0)
        vg = v_ref[:, lo : lo + wide]
        full = lax.dot_general(kg, vg, (((0,), (0,)), ((), ())), preferred_element_type=f32)
        head = lax.broadcasted_iota(jnp.int32, (HD, wide), 1) // HD
        small = full[:HD]
        for h in range(1, wide // HD):
            small = jnp.where(head == h, full[h * HD : (h + 1) * HD], small)
        sums = jnp.dot(ones, kg, preferred_element_type=f32)
        where = pl.ds((g % per_half) * LANES, wide)
        state[g // per_half, :, where] = small
        row = g % per_half
        state[g // per_half, row : row + 1, half : half + wide] = sums[:1]

    band_out[...] = pack(state[ob])
    swap = remote(band_out, band_in, s_send.at[0], s_recv.at[0], at(y, t, ob))
    swap.start()
    sends.append((None, swap))

    loads[2].wait()
    size = flat_ref.shape[2]
    for lo in range(0, size, 8 * LANES):
        wide = min(8 * LANES, size - lo)
        chunks_ref[lo // LANES : (lo + wide) // LANES, :] = (
            flat_ref[0, :, lo : lo + wide].astype(f32).reshape(wide // LANES, LANES)
        )
    pairs, per_pair, tiles = shard_rows // 2, 2 * depth // LANES, -(-depth // LANES)
    w_wide[...] = jnp.zeros_like(w_wide)
    lower = lax.broadcasted_iota(jnp.int32, (pairs, LANES), 1) < LANES // 2

    def chunk(j):
        return chunks_ref[pl.ds(j, pairs, stride=per_pair), :]

    middle = chunk(tiles - 1)
    for j in range(tiles - 1):
        w_wide[j, pl.ds(0, pairs, stride=2), :] = chunk(j)
    w_wide[tiles - 1, pl.ds(0, pairs, stride=2), :] = jnp.where(lower, middle, 0.0)
    turned = pltpu.roll(middle, LANES // 2, 1)
    for j in range(tiles):
        if j + 1 < tiles:
            following = pltpu.roll(chunk(tiles + j), LANES // 2, 1)
        else:
            following = jnp.zeros_like(turned)
        w_wide[j, pl.ds(1, pairs, stride=2), :] = jnp.where(lower, turned, following)
        turned = following
    for j in range(w_wide.shape[0]):
        w_ref[:, j * LANES : (j + 1) * LANES] = w_wide[j].astype(bf16)
    for condition, copy in locals_:
        pl.when(condition)(copy.start)
    swap.wait_recv()
    own[...] = state[b] + unpack(band_in[...])

    for s in range(hops):
        d = 1 << s
        hop = remote(
            hop_out.at[s], hop_in.at[s], s_send.at[1 + s], s_recv.at[1 + s],
            at(y, lax.rem(t + d, n), b),
        )
        hop_out[s] = pack(own[...])

        @pl.when(t + d < n)
        def _():
            hop.start()

        sends.append((t + d < n, hop))
        if s == 0:
            first_step(b)
        elif s == 1:
            first_step(ob)
            w_put(own_rows, me_slot, t, ob)
        elif s == 2:
            forward(1, (b,))

        @pl.when(t >= d)
        def _():
            hop.wait_recv()
            own[...] += unpack(hop_in[s])

    final[b] = pack(own[...])
    swap = remote(final.at[b], final.at[b], s_send.at[1 + hops], s_recv.at[1 + hops], at(y, t, ob))
    swap.start()
    sends.append((None, swap))
    forward(1, (ob,))
    arrived += [chip(pos - 1), chip(pos + 1)]
    swap.wait_recv()

    loads[3].wait()
    loads[4].wait()
    partner_slot, far_slot, far_partner = y * 2 + ob, oy * 2 + b, oy * 2 + ob
    shards, few = 2 * n, shard_rows - main
    part = tokens // 2

    def piece(slot, h):
        return abuf.at[slot, pl.ds(h * part, part), :]

    def a_put(slot, h, i, peer):
        view = piece(slot, h)
        copy = remote(view, view, a_send.at[i, h], a_recv.at[slot, h], peer)
        copy.start()
        sends.append((None, copy))

    def a_wait(slot, h):
        view = piece(slot, h)
        remote(view, view, a_send.at[0, h], a_recv.at[slot, h], at(y, t, ob)).wait_recv()

    for h in range(2):
        top = h * part
        total = jnp.zeros((part, 1), f32)
        for g in range(groups):
            lo, wide = g * LANES, min(LANES, depth - g * LANES)
            row = g % per_half
            qg = jnp.maximum(q_ref[top : top + part, lo : lo + wide], 0)
            small = final[g // per_half, :, pl.ds(row * LANES, wide)].astype(f32)
            same = (
                lax.broadcasted_iota(jnp.int32, (wide, wide), 0) // HD
                == lax.broadcasted_iota(jnp.int32, (wide, wide), 1) // HD
            )
            tall = jnp.concatenate([small] * (wide // HD), axis=0)
            numer = jnp.dot(qg, jnp.where(same, tall, 0.0).astype(bf16), preferred_element_type=f32)
            sums = final[g // per_half, :, half : half + wide].astype(f32)
            weigh = sums[row : row + 1] + sums[rows + row : rows + row + 1]
            terms = qg.astype(f32) * weigh
            hi = terms.astype(bf16)
            rest = (terms - hi.astype(f32)).astype(bf16)
            block_ones = jnp.where(same, 1.0, 0.0).astype(bf16)
            both = jnp.concatenate([hi, rest], axis=0)
            denom = jnp.dot(both, block_ones, preferred_element_type=f32)
            r = numer / (denom[:part] + denom[part:] + read_epsilon)
            reads[top : top + part, lo : lo + wide] = r
            total = total + jnp.sum(r * r, axis=-1, keepdims=True)
        scale = lax.rsqrt(total * (1.0 / depth) + norm_epsilon)
        normed = reads[top : top + part, :] * scale * g_ref[...][None, :]
        gap = jnp.zeros((part, wrest.shape[1] - few), f32)
        extra = []
        for slot in range(shards):
            lo = (slot % 2 * n + slot // 2) * shard_rows
            abuf[mine, top : top + part, slot * main : (slot + 1) * main] = normed[
                :, lo : lo + main
            ].astype(bf16)
            extra += [normed[:, lo + main : lo + shard_rows], gap]
        abuf[mine, top : top + part, shards * main :] = jnp.concatenate(extra, axis=1).astype(bf16)
        a_put(mine, h, 0, at(oy, t, b))
        a_put(mine, h, 1, at(y, t, ob))
        forward(2, ((b, ob)[h],))

    arrived += [chip(pos - 2), chip(pos + 2)]
    acc[...] = jnp.zeros_like(acc)
    for condition, copy in locals_:
        pl.when(condition)(copy.wait)
    w_wait(2 * t + ob)
    arrived.append(t)

    def add(p, side):
        lanes = pl.ds(pl.multiple_of(p * 2 * main, LANES), 2 * main)
        both = abuf[pl.ds(2 * side, 2), :, lanes].reshape(2 * tokens, 2 * main)
        rows = wbuf[pl.ds(2 * p, 2)].reshape(2 * main, block)
        acc[side] += jnp.dot(both, rows, preferred_element_type=f32)

    def add_rest(side):
        both = abuf[pl.ds(2 * side, 2), :, shards * main :].reshape(2 * tokens, -1)
        rows = wrest[...].reshape(-1, block)
        acc[side] += jnp.dot(both, rows, preferred_element_type=f32)

    for h in range(2):
        a_wait(partner_slot, h)
    early = len(arrived)
    for p in arrived:
        add(p, y)
    for s in range(3, n // 2):
        forward(s)
    for h in range(2):
        a_wait(far_slot, h)
        a_put(far_slot, h, 2, at(y, t, ob))
    for p in arrived[early:]:
        add(p, y)
    for h in range(2):
        a_wait(far_partner, h)
    for p in arrived:
        add(p, oy)
    arrived.clear()
    forward(n // 2)

    def rows_of(side, pb):
        return acc[side, pl.ds(pl.multiple_of(pb * tokens, 8), tokens), :].astype(bf16)

    def give(i, side, pb):
        res_out[i] = rows_of(side, pb)
        for core in range(2):
            lanes = pl.ds(0, widths[core])
            copy = remote(
                res_out.at[i, :, lanes], res_in.at[mine, :, lanes],
                r_send.at[i], r_recv.at[mine], at(side, t, pb),
            )
            pl.when(b == core)(copy.start)
            sends.append((b == core, copy))

    def take(slot, core):
        view = res_in.at[slot, :, pl.ds(0, widths[core])]
        remote(view, view, r_send.at[0], r_recv.at[slot], at(y, t, ob)).wait_recv()

    add(arrived[0], oy)
    add_rest(oy)
    give(0, oy, b)
    give(1, oy, ob)
    add(arrived[0], y)
    add_rest(y)
    give(2, y, ob)
    res_in[mine] = rows_of(y, b)
    for slot, pb in ((partner_slot, ob), (far_slot, b), (far_partner, ob)):
        for core in range(2):
            pl.when(pb == core)(functools.partial(take, slot, core))
    for c in range(4):
        start = c // 2 * sum(widths) + c % 2 * widths[0]
        wide = min(widths[c % 2], depth - start)
        out_ref[:, start : start + wide] = res_in[c, :, :wide]
    for condition, copy in sends:
        if condition is None:
            copy.wait_send()
        else:
            pl.when(condition)(copy.wait_send)


def fast_body(n, query_tokens, key_tokens, value_tokens, norm_gain, out_weight):
    frames, rows, width, depth = query_tokens.shape
    tokens = frames * rows * width
    shard_rows = out_weight.size // depth
    padded = round_up(shard_rows, 16)
    block = core_widths(depth)[0]
    half = round_up(-(-depth // 2), LANES)
    hops = n.bit_length() - 1
    main = shard_rows // LANES * LANES
    rest = padded - main
    wide = 2 * sum(core_widths(depth))
    flat = [x.reshape(tokens, depth) for x in (query_tokens, key_tokens, value_tokens)]
    f32, bf16 = jnp.float32, jnp.bfloat16
    packed = half + LANES
    dma = pltpu.SemaphoreType.DMA
    out = pl.pallas_call(
        functools.partial(kernel, n, shard_rows),
        out_shape=jax.ShapeDtypeStruct((tokens, depth), bf16),
        in_specs=[pl.BlockSpec(memory_space=pltpu.HBM)] * 5,
        out_specs=pl.BlockSpec(memory_space=pltpu.VMEM),
        scratch_shapes=[
            *[pltpu.VMEM((tokens, depth), bf16)] * 3,
            pltpu.VMEM((depth,), f32),
            pltpu.VMEM(out_weight.shape, bf16),
            dma((5,)),
            pltpu.VMEM((out_weight.size // LANES, LANES), f32),
            pltpu.VMEM((wide // LANES, padded, LANES), f32),
            pltpu.VMEM((padded, wide), bf16),
            pltpu.VMEM((2, HD, packed), f32),
            pltpu.VMEM((HD, packed), f32),
            pltpu.VMEM((HD, packed), bf16),
            pltpu.VMEM((HD, packed), bf16),
            pltpu.VMEM((hops, HD, packed), bf16),
            pltpu.VMEM((hops, HD, packed), bf16),
            pltpu.VMEM((2, HD, packed), bf16),
            pltpu.VMEM((tokens, depth), f32),
            pltpu.VMEM((2 * n, main, block), bf16),
            pltpu.VMEM((2 * n, rest, block), bf16),
            pltpu.VMEM((4, tokens, 2 * n * padded), bf16),
            pltpu.VMEM((2, 2 * tokens, block), f32),
            pltpu.VMEM((3, tokens, block), bf16),
            pltpu.VMEM((4, tokens, block), bf16),
            dma((2,)),
            dma((2 * n + 8,)),
            dma((2 * n,)),
            dma((2 * n + 8,)),
            dma((2 * n,)),
            dma((hops + 2,)),
            dma((hops + 2,)),
            dma((3, 2)),
            dma((4, 2)),
            dma((3,)),
            dma((4,)),
        ],
        compiler_params=pltpu.CompilerParams(
            collective_id=0, has_side_effects=True, vmem_limit_bytes=63 * 1024 * 1024
        ),
    )(*flat, norm_gain, out_weight)
    return out.reshape(query_tokens.shape)


def solution(mesh):
    n, bands, parts = mesh.shape["tm"], mesh.shape["band"], mesh.shape["parts"]

    def body(query_tokens, key_tokens, value_tokens, norm_gain, out_weight):
        depth = query_tokens.shape[3]
        ring = n >= 8 and n & (n - 1) == 0 and bands == 2 and parts == 2
        whole_pairs = out_weight.size % (2 * depth) == 0 and depth % LANES == LANES // 2
        few = round_up(-(-depth // 2), LANES) // LANES <= HD // 2
        ring = ring and LANES < out_weight.size // depth
        if ring and query_tokens.shape[0] == 1 and whole_pairs and few:
            return fast_body(n, query_tokens, key_tokens, value_tokens, norm_gain, out_weight)
        return plain_body(query_tokens, key_tokens, value_tokens, norm_gain, out_weight)

    spread = P(("parts", "tm"), "band", None, None)
    return jax.shard_map(
        body,
        mesh=mesh,
        in_specs=(spread, spread, spread, P(), P("band", "tm", None)),
        out_specs=spread,
        check_vma=False,
    )
```
